512 devices in a mesh: seq: 32 (over y_lo, z), mp: 16 (over x, y_hi, core).
Axes of the slice: x: 4, y: 4 (y_hi: 2, y_lo: 2; y = y_hi * 2 + y_lo), z: 16, core: 2. Of those that a mesh axis runs over, the one named last changes fastest.
Arguments:
- tokens: bfloat16 [8192, 2048], P('seq', 'mp'), may hold values from -6 to 6
- norm_gain: float32 [2048], replicated, may hold values from 0.1 to 1.9
- w_query: bfloat16 [2048, 2048], P('seq', 'mp'), may hold values from -0.75 to 0.75
- w_key: bfloat16 [2048, 2048], P('seq', 'mp'), may hold values from -0.75 to 0.75
- w_value: bfloat16 [2048, 2048], P('seq', 'mp'), may hold values from -0.125 to 0.125
- w_out: bfloat16 [2048, 2048], P('seq', 'mp'), may hold values from -0.125 to 0.125
- head_slope: float32 [16], replicated, may hold values from 0.01 to 0.5
- segment_ids: int32 [8192], P('seq'), may hold values from 0 to 31, never falling along the last dimension, each value on 1 to 1024 neighbouring positions
Outputs:
- mixed: bfloat16 [8192, 2048], P('seq', 'mp')
The draws below stay inside these ranges and needn't reach their ends.
Inputs may be any that keep to these rules, and one draw needn't show every extreme that they name: `segment_ids`: homolog numbers never fall along the tokens; every number names 1 to 1024 consecutive tokens, and one names exactly 1024.
All inputs are finite; a program needn't handle non-finite values.
Results may differ from the reference program's by a relative error of at most 0.0055.
Values may be sent and summed in bfloat16 or wider, within the bound.
A program may use at most 64 MiB of HBM per device.

```python
import math
import jax
import jax.numpy as jnp
import numpy as np
from jax import lax

D = 2048
HEADS = 16
SEG_MAX = 1024
TOKENS = 8192
SEGS = 32


def shared_base(key):
    return jnp.clip(jax.random.normal(key, (D, D), jnp.float32), -3.0, 3.0)


def draw_w_query(key, part):
    base = shared_base(key)
    scaled = base * 1.7
    return (scaled / math.sqrt(D)).astype(jnp.bfloat16)


def draw_w_key(key, part):
    key = jax.random.fold_in(key, 11)
    own_part = jnp.clip(jax.random.normal(key, (D, D), jnp.float32), -3.0, 3.0)
    scaled = 1.7 * own_part
    return (scaled / math.sqrt(D)).astype(jnp.bfloat16)


def block_levels(rng, shape, pieces, low, high):
    loudness, own = 1.0, jax.random.fold_in(rng, 6)
    for axis_at, shards_of in pieces:
        steps = jnp.exp(jax.random.uniform(jax.random.fold_in(own, axis_at), (shards_of,), jnp.float32, low / len(pieces), high / len(pieces)))
        loudness = loudness * jnp.repeat(steps, shape[axis_at] // shards_of).reshape([-1 if axis == axis_at else 1 for axis in range(len(shape))])
    return loudness


def split_up(number_of, total, reach, lean):
    weights = [(1 << 20) // math.isqrt(grade ** lean) + 1 for grade in range(2, number_of + 1)]
    surplus, holding = total - reach - (number_of - 1), [1] * (number_of - 1)
    while surplus > 0:
        movable = [i for i in range(number_of - 1) if holding[i] < reach]
        mass, budget = sum([weights[i] for i in movable]), surplus
        for i in movable:
            more = min(reach - holding[i], max(1, budget * weights[i] // mass), surplus)
            holding[i] = holding[i] + more
            surplus = surplus - more
    return np.array([reach] + holding)


def uneven_parts(rng, amount, total, most, skew):
    if amount == 2:
        one = jax.random.randint(rng, (), max(1, total - most), min(most, total - 1) + 1)
        return jnp.stack([one, total - one])
    tallies = jnp.asarray(split_up(amount, total, most, skew), jnp.int32)
    pairs = (amount - 1) // 2
    source_of, receiver = tallies[1:1 + 2 * pairs:2], tallies[2:2 + 2 * pairs:2]
    margin = jnp.minimum(source_of - 1, most - receiver)
    moved = jax.random.randint(jax.random.fold_in(rng, 1), (pairs,), 0, 1 << 20) % (margin + 1)
    tallies = tallies.at[1:1 + 2 * pairs:2].set(source_of - moved).at[2:2 + 2 * pairs:2].set(receiver + moved)
    return tallies[jax.random.permutation(jax.random.fold_in(rng, 2), amount)]


def bell_draw(stream_key, shape, spread, bound, shards=(), held_as=jnp.bfloat16):
    result = jax.random.normal(stream_key, shape, jnp.float32) * spread
    if len(shards) > 0:
        result = block_levels(stream_key, shape, shards, -0.22, 0.18) * result
    return jnp.clip(result, min=-bound, max=bound).astype(held_as)


def setup_inputs(seed: int = 0) -> dict:
    seeds = jax.random.split(jax.random.key(seed), 9)
    tokens = bell_draw(seeds[0], (TOKENS, D), 1.0, 6.0, ((0, 32), (1, 16)))
    norm_gain = jnp.clip(1.0 + 0.18 * jax.random.normal(seeds[1], (D,), jnp.float32), 0.1, 1.9)
    w_query = draw_w_query(jax.random.fold_in(seeds[8], 71), 0)
    w_key = draw_w_key(jax.random.fold_in(seeds[8], 71), 0)
    w_value = bell_draw(seeds[4], (D, D), D ** -0.5, 0.125, ((0, 32), (1, 16)))
    w_out = bell_draw(seeds[5], (D, D), D ** -0.5, 0.125, ((0, 32), (1, 16)))
    head_slope = jnp.clip(jnp.exp(jax.random.uniform(seeds[6], (HEADS,), jnp.float32, math.log(0.01), math.log(0.5))), 0.01, 0.5)
    segment_ids = jnp.searchsorted(jnp.cumsum(uneven_parts(seeds[7], SEGS, TOKENS, SEG_MAX, 2)), jnp.arange(TOKENS), side="right").astype(jnp.int32)
    return {"tokens": tokens, "norm_gain": norm_gain, "w_query": w_query, "w_key": w_key, "w_value": w_value, "w_out": w_out, "head_slope": head_slope, "segment_ids": segment_ids}


EPSILON = 1e-05
MASKED_SCORE = -1e+30

def reference(tokens, norm_gain, w_query, w_key, w_value, w_out, head_slope, segment_ids):
    stream = tokens.astype(jnp.float32)
    mean_square = lax.optimization_barrier(jnp.mean(stream * stream, axis=1, keepdims=True))
    normed = (stream * lax.rsqrt(mean_square + EPSILON) * norm_gain).astype(jnp.bfloat16)
    query_proj = jnp.dot(normed, w_query, preferred_element_type=jnp.float32).astype(jnp.bfloat16)
    key_proj = jnp.dot(normed, w_key, preferred_element_type=jnp.float32).astype(jnp.bfloat16)
    value_proj = jnp.dot(normed, w_value, preferred_element_type=jnp.float32).astype(jnp.bfloat16)
    head_width = D // HEADS
    inv_scale = 1.0 / math.sqrt(head_width)
    positions = jnp.arange(TOKENS, dtype=jnp.int32)
    seg_float = segment_ids.astype(jnp.float32)
    block_rows = min(512, TOKENS)
    outputs = []
    for block_index in range(TOKENS // block_rows):
        first_row = block_index * block_rows
        last_row = first_row + block_rows
        query_heads = query_proj[first_row:last_row].reshape(block_rows, HEADS, head_width).transpose(1, 0, 2)
        key_heads = key_proj[:last_row].reshape(last_row, HEADS, head_width).transpose(1, 0, 2)
        value_heads = value_proj[:last_row].reshape(last_row, HEADS, head_width).transpose(1, 0, 2)
        allowed = positions[:last_row][None, :] <= positions[first_row:last_row][:, None]
        seg_gap = seg_float[first_row:last_row][:, None] - seg_float[:last_row][None, :]

        def one_head(operands):
            query_one, key_one, value_one, slope = operands
            scores = jnp.dot(query_one, key_one.T, preferred_element_type=jnp.float32) * inv_scale - slope * seg_gap
            scores = jnp.where(allowed, scores, MASKED_SCORE)
            row_max = lax.optimization_barrier(jnp.max(scores, axis=1, keepdims=True))
            weights = jnp.where(allowed, jnp.exp(scores - row_max), 0.0)
            denominator = lax.optimization_barrier(jnp.sum(weights, axis=1, keepdims=True))
            weighted = jnp.dot(weights.astype(jnp.bfloat16), value_one, preferred_element_type=jnp.float32)
            return weighted / denominator
        heads_out = lax.map(one_head, (query_heads, key_heads, value_heads, head_slope))
        outputs.append(heads_out.transpose(1, 0, 2).reshape(block_rows, D).astype(jnp.bfloat16))
    attended = jnp.concatenate(outputs, axis=0)
    projected = jnp.dot(attended, w_out, preferred_element_type=jnp.float32)
    return (stream + projected).astype(jnp.bfloat16)
```

```python
import functools
import math

import jax
import jax.numpy as jnp
from jax import lax
from jax.experimental import pallas as pl
from jax.experimental.pallas import tpu as pltpu
from jax.sharding import PartitionSpec as P

EPSILON = 1e-05
MASKED_SCORE = -1e30
MESH = pl.DeviceIdType.MESH


def remote(src, dst, send, recv, device):
    return pltpu.make_async_remote_copy(
        src_ref=src, dst_ref=dst, send_sem=send, recv_sem=recv, device_id=device, device_id_type=MESH
    )


def kernel(
    nz, nx, ny, tok, gain, wq, wk, wv, wo, slopes, seg, out,
    xg, nb, wg, kt, vb, qb, mb, lb, ab, ob, sb, att,
    tok_s, tok_r, w_s, w_r, wy_s, wy_r, k_s, k_r, v_s, v_r, x_s, x_r, a_s, a_r, f_s, f_r,
):
    rows, hw = tok.shape
    depth = wq.shape[0]
    nm = nx * ny * 2
    up_steps = nz // 2
    down_steps = nz - 1 - up_steps
    s = lax.axis_index("seq")
    m = lax.axis_index("mp")
    z = lax.rem(s, nz)
    yl = lax.div(s, nz)
    core = lax.rem(m, 2)
    yh = lax.rem(lax.div(m, 2), ny)
    x = lax.div(m, 2 * ny)

    def ring(place):
        return lax.rem(place + nz, nz)

    up = {"seq": yl * nz + ring(z + 1), "mp": m}
    down = {"seq": yl * nz + ring(z - 1), "mp": m}
    across = {"seq": (1 - yl) * nz + z, "mp": m}
    sibling = {"seq": s, "mp": m + 1 - 2 * core}

    def mp_at(index, sign, flip):
        a, b = index // ny, index % ny
        ox = lax.rem(x + (a if sign > 0 else nx - a), nx)
        oy = lax.rem(yh + (b if sign > 0 else ny - b), ny)
        oc = 1 - core if flip else core
        return (ox * ny + oy) * 2 + oc

    barrier = pltpu.get_barrier_semaphore()
    greeted = [up, down, across]
    for flip in (False, True):
        for index in range(nx * ny):
            if index or flip:
                greeted.append({"seq": s, "mp": mp_at(index, 1, flip)})
    for device in greeted:
        pl.semaphore_signal(barrier, inc=1, device_id=device, device_id_type=MESH)

    def shard(owner):
        return wg.at[pl.ds(pl.multiple_of(owner * depth, depth), depth), :]

    own_rows = pl.ds(pl.multiple_of(s * depth, depth), depth)
    for index, weight in enumerate((wq, wk, wv, wo)):
        wg[own_rows, index * hw:(index + 1) * hw] = weight[...]
    xg[m] = tok[...]
    pl.semaphore_wait(barrier, len(greeted))

    def w_up(step):
        ref = shard(yl * nz + ring(z - step + 1))
        return remote(ref, ref, w_s.at[0, step], w_r.at[0, step], up)

    def w_down(step):
        ref = shard(yl * nz + ring(z + step - 1))
        return remote(ref, ref, w_s.at[1, step], w_r.at[1, step], down)

    def w_across(way, step):
        ref = shard(yl * nz + ring(z - step if way == 0 else z + step))
        return remote(ref, ref, wy_s.at[way, step], wy_r.at[way, step], across)

    def w_across_in(way, step):
        ref = shard((1 - yl) * nz + ring(z - step if way == 0 else z + step))
        return remote(ref, ref, wy_s.at[way, step], wy_r.at[way, step], across)

    def w_up_in(step):
        ref = shard(yl * nz + ring(z - step))
        return remote(ref, ref, w_s.at[0, step], w_r.at[0, step], up)

    def w_down_in(step):
        ref = shard(yl * nz + ring(z + step))
        return remote(ref, ref, w_s.at[1, step], w_r.at[1, step], down)

    w_up(1).start()
    w_down(1).start()
    w_across(0, 0).start()

    partners = []
    for flip in (True, False):
        for index in range(nx * ny):
            if index or flip:
                partners.append((len(partners), index, flip))

    def tok_out(slot, index, flip):
        return remote(tok, xg.at[m], tok_s.at[slot], tok_r.at[slot], {"seq": s, "mp": mp_at(index, 1, flip)})

    def tok_in(slot, index, flip):
        ref = xg.at[mp_at(index, -1, flip)]
        return remote(ref, ref, tok_s.at[slot], tok_r.at[slot], sibling)

    for partner in partners:
        tok_out(*partner).start()

    def w_step(step, carry):
        w_up_in(step).wait_recv()

        @pl.when(step < up_steps)
        def _():
            w_up(step + 1).start()

        @pl.when(step <= down_steps)
        def _():
            w_down_in(step).wait_recv()

            @pl.when(step < down_steps)
            def _():
                w_down(step + 1).start()

        w_across(0, step).start()

        @pl.when(step <= down_steps)
        def _():
            w_across(1, step).start()

        return carry

    middle = up_steps // 2 + 1
    lax.fori_loop(1, middle + 1, w_step, 0)

    for partner in partners:
        tok_in(*partner).wait_recv()
    square = jnp.zeros((rows, hw), jnp.float32)
    for h in range(nm):
        part = xg[h].astype(jnp.float32)
        square = square + part * part
    mean = jnp.sum(square, axis=1, keepdims=True) * (1.0 / (nm * hw))
    scale = jnp.broadcast_to(lax.rsqrt(mean + EPSILON), (rows, hw))
    for h in range(nm):
        part = xg[h].astype(jnp.float32) * scale * gain[:, h * hw:(h + 1) * hw]
        nb[:, h * hw:(h + 1) * hw] = part.astype(jnp.bfloat16)

    lax.fori_loop(middle + 1, up_steps + 1, w_step, 0)

    def across_in(step, carry):
        w_across_in(0, step).wait_recv()

        @pl.when((step >= 1) & (step <= down_steps))
        def _():
            w_across_in(1, step).wait_recv()

        return carry

    lax.fori_loop(0, up_steps + 1, across_in, 0)

    proj = jnp.dot(nb[...], wg[:, :3 * hw], preferred_element_type=jnp.float32)
    qb[1] = proj[:, :hw].astype(jnp.bfloat16)
    kt[z, :hw, :] = jnp.transpose(proj[:, hw:2 * hw]).astype(jnp.bfloat16)
    kt[z, hw:hw + 16, :] = jnp.broadcast_to(seg[...].astype(jnp.float32), (16, rows)).astype(jnp.bfloat16)
    vb[z] = proj[:, 2 * hw:].astype(jnp.bfloat16)

    def kv_out(buf, ss, rs, way, step):
        ref = buf.at[ring(z - step + 1 if way == 0 else z + step - 1)]
        return remote(ref, ref, ss.at[way, step], rs.at[way, step], up if way == 0 else down)

    def kv_in(buf, ss, rs, way, step):
        ref = buf.at[ring(z - step if way == 0 else z + step)]
        return remote(ref, ref, ss.at[way, step], rs.at[way, step], up if way == 0 else down)

    key_side, value_side = (kt, k_s, k_r), (vb, v_s, v_r)
    for side in (key_side, value_side):
        kv_out(*side, 0, 1).start()
        kv_out(*side, 1, 1).start()

    query_copy = remote(qb.at[1], qb.at[0], x_s.at[0], x_r.at[0], across)

    @pl.when(yl == 1)
    def _():
        query_copy.start()

    slope = slopes[m]
    inv_scale = 1.0 / math.sqrt(hw)
    mb[...] = jnp.full(mb.shape, MASKED_SCORE, jnp.float32)
    lb[...] = jnp.zeros(lb.shape, jnp.float32)
    ab[...] = jnp.zeros(ab.shape, jnp.float32)

    def attend(group, block):
        bias = kt[block, hw:hw + 16, :].astype(jnp.float32)[:1, :] * slope
        scores = jnp.dot(qb[group], kt[block, :hw, :], preferred_element_type=jnp.float32)
        scores = scores * inv_scale + bias
        reach = jnp.where(group == 0, nz * rows, (z - block) * rows)
        row = lax.broadcasted_iota(jnp.int32, scores.shape, 0)
        col = lax.broadcasted_iota(jnp.int32, scores.shape, 1)
        scores = jnp.where(col - row <= reach, scores, MASKED_SCORE)
        old = mb[group]
        new = jnp.maximum(old, jnp.max(scores, axis=1, keepdims=True))
        weights = jnp.exp(scores - jnp.concatenate([new] * (rows // hw), axis=1))
        factor = jnp.exp(old - new)
        total = lb[group] * factor
        for part in range(rows // hw):
            total = total + weights[:, part * hw:(part + 1) * hw]
        mb[group] = new
        lb[group] = total
        ab[group] = ab[group] * factor + jnp.dot(
            weights.astype(jnp.bfloat16), vb[block], preferred_element_type=jnp.float32
        )

    def kv_step(step, carry):
        for side in (key_side, value_side):
            for way, last in ((0, up_steps), (1, down_steps)):
                @pl.when((step >= 1) & (step <= last))
                def _():
                    kv_in(*side, way, step).wait_recv()

                    @pl.when(step < last)
                    def _():
                        kv_out(*side, way, step + 1).start()

        def task(index, inner):
            way, group = lax.div(index, 2), 1 - lax.rem(index, 2)
            block = ring(jnp.where(way == 0, z - step, z + step))

            @pl.when((index == 1) & (step == 0) & (yl == 0))
            def _():
                query_copy.wait_recv()

            wanted = jnp.where(group == 0, yl == 0, block <= z)
            exists = (way == 0) | ((step >= 1) & (step <= down_steps))

            @pl.when(wanted & exists)
            def _():
                attend(group, block)

            return inner

        lax.fori_loop(0, 4, task, 0)

        w_across(0, step).wait_send()

        @pl.when(step >= 1)
        def _():
            w_up(step).wait_send()

        @pl.when((step >= 1) & (step <= down_steps))
        def _():
            w_down(step).wait_send()
            w_across(1, step).wait_send()

        return carry

    lax.fori_loop(0, up_steps + 1, kv_step, 0)

    out_copy = remote(ob.at[0], ob.at[1], x_s.at[1], x_r.at[1], across)
    stat_copy = remote(sb.at[0], sb.at[1], x_s.at[2], x_r.at[2], across)

    @pl.when(yl == 0)
    def _():
        total = jnp.sum(lb[0], axis=1, keepdims=True)
        ob[0] = (ab[0] / total).astype(jnp.bfloat16)
        level = jnp.broadcast_to(mb[0] + jnp.log(total), (rows, hw))
        sb[0] = jnp.transpose(level)[:8, :]
        out_copy.start()
        stat_copy.start()

    total = jnp.sum(lb[1], axis=1, keepdims=True)
    own = ab[1] / total

    @pl.when(yl == 0)
    def _():
        att[m] = own.astype(jnp.bfloat16)

    @pl.when(yl == 1)
    def _():
        out_copy.wait_recv()
        stat_copy.wait_recv()
        other_level = jnp.transpose(jnp.broadcast_to(sb[1][:1, :], (hw, rows)))
        own_level = jnp.broadcast_to(mb[1] + jnp.log(total), (rows, hw))
        share = 1.0 / (1.0 + jnp.exp(other_level - own_level))
        merged = own * share + ob[1].astype(jnp.float32) * (1.0 - share)
        att[m] = merged.astype(jnp.bfloat16)

    def att_out(index):
        ref = att.at[m]
        return remote(ref, ref, a_s.at[index], a_r.at[index], {"seq": s, "mp": mp_at(index, 1, False)})

    def att_in(index):
        ref = att.at[mp_at(index, -1, False)]
        return remote(ref, ref, a_s.at[index], a_r.at[index], sibling)

    def hand_out(index):
        ref = att.at[mp_at(index, -1, False)]
        return remote(ref, ref, f_s.at[index], f_r.at[index], sibling)

    def hand_in(index):
        ref = att.at[mp_at(index, -1, True)]
        return remote(ref, ref, f_s.at[index], f_r.at[index], sibling)

    chips = nx * ny
    for index in reversed(range(1, chips)):
        att_out(index).start()
    hand_out(0).start()

    def kv_sent(step, carry):
        for side in (key_side, value_side):
            kv_out(*side, 0, step).wait_send()

            @pl.when(step <= down_steps)
            def _():
                kv_out(*side, 1, step).wait_send()

        return carry

    lax.fori_loop(1, up_steps + 1, kv_sent, 0)
    for partner in partners:
        tok_out(*partner).wait_send()

    @pl.when(yl == 1)
    def _():
        query_copy.wait_send()

    @pl.when(yl == 0)
    def _():
        out_copy.wait_send()
        stat_copy.wait_send()

    for index in range(1, chips):
        att_in(index).wait_recv()
        hand_out(index).start()
    for index in range(chips):
        hand_in(index).wait_recv()

    mixed = tok[...].astype(jnp.float32)
    for pair in range(nm // 2):
        left = jnp.concatenate([att[2 * pair], att[2 * pair + 1]], axis=1)
        right = wg[2 * pair * hw:(2 * pair + 2) * hw, 3 * hw:]
        mixed = mixed + jnp.dot(left, right, preferred_element_type=jnp.float32)
    out[...] = mixed.astype(jnp.bfloat16)

    for index in range(1, chips):
        att_out(index).wait_send()
    for index in range(chips):
        hand_out(index).wait_send()


def on_device(nz, nx, ny, tokens, norm_gain, w_query, w_key, w_value, w_out, head_slope, segment_ids):
    rows, hw = tokens.shape
    depth = w_query.shape[0]
    nm = nx * ny * 2
    steps = nz // 2 + 1
    vmem = pl.BlockSpec(memory_space=pltpu.VMEM)
    dma = pltpu.SemaphoreType.DMA
    return pl.pallas_call(
        functools.partial(kernel, nz, nx, ny),
        out_shape=jax.ShapeDtypeStruct((rows, hw), jnp.bfloat16),
        in_specs=[vmem] * 6 + [pl.BlockSpec(memory_space=pltpu.SMEM), vmem],
        out_specs=vmem,
        scratch_shapes=[
            pltpu.VMEM((nm, rows, hw), jnp.bfloat16),
            pltpu.VMEM((rows, nm * hw), jnp.bfloat16),
            pltpu.VMEM((2 * nz * depth, 4 * hw), jnp.bfloat16),
            pltpu.VMEM((nz, hw + 16, rows), jnp.bfloat16),
            pltpu.VMEM((nz, rows, hw), jnp.bfloat16),
            pltpu.VMEM((2, rows, hw), jnp.bfloat16),
            pltpu.VMEM((2, rows, hw), jnp.float32),
            pltpu.VMEM((2, rows, hw), jnp.float32),
            pltpu.VMEM((2, rows, hw), jnp.float32),
            pltpu.VMEM((2, rows, hw), jnp.bfloat16),
            pltpu.VMEM((2, 8, rows), jnp.float32),
            pltpu.VMEM((nm, rows, hw), jnp.bfloat16),
            dma((nm - 1,)), dma((nm - 1,)),
            dma((2, steps)), dma((2, steps)),
            dma((2, steps)), dma((2, steps)),
            dma((2, steps)), dma((2, steps)),
            dma((2, steps)), dma((2, steps)),
            dma((3,)), dma((3,)),
            dma((nx * ny,)), dma((nx * ny,)),
            dma((nx * ny,)), dma((nx * ny,)),
        ],
        compiler_params=pltpu.CompilerParams(
            collective_id=0, has_side_effects=True, vmem_limit_bytes=40 << 20
        ),
        name="sublayer",
    )(
        tokens, norm_gain.reshape(1, -1), w_query, w_key, w_value, w_out, head_slope,
        segment_ids.reshape(1, -1),
    )


def solution(mesh):
    nz = mesh.shape["seq"] // 2
    ny = 2
    nx = mesh.shape["mp"] // (2 * ny)
    return jax.shard_map(
        functools.partial(on_device, nz, nx, ny),
        mesh=mesh,
        in_specs=(
            P("seq", "mp"), P(), P("seq", "mp"), P("seq", "mp"),
            P("seq", "mp"), P("seq", "mp"), P(), P("seq"),
        ),
        out_specs=P("seq", "mp"),
        check_vma=False,
    )
```

```python
import functools
import math

import jax
import jax.numpy as jnp
from jax import lax
from jax.experimental import pallas as pl
from jax.experimental.pallas import tpu as pltpu
from jax.sharding import PartitionSpec as P

EPSILON = 1e-05
MASKED_SCORE = -1e30
MESH = pl.DeviceIdType.MESH


def remote(src, dst, send, recv, device):
    return pltpu.make_async_remote_copy(
        src_ref=src, dst_ref=dst, send_sem=send, recv_sem=recv, device_id=device, device_id_type=MESH
    )


def kernel(
    nz, nx, ny, tok, gain, wq, wk, wv, wo, slopes, seg, out,
    xg, nb, wg, gv, sv, kt, vb, qb, mb, lb, ab, ob, sb, att,
    l_s, o_s, o_r, tok_s, tok_r, w_s, w_r, wy_s, wy_r, kv_s, kv_r, x_s, x_r, a_s, a_r, f_s, f_r,
):
    rows, hw = tok.shape
    depth = wq.shape[0]
    nm = nx * ny * 2
    up_steps = nz // 2
    down_steps = nz - 1 - up_steps
    jump = 5
    s = lax.axis_index("seq")
    m = lax.axis_index("mp")
    z = lax.rem(s, nz)
    yl = lax.div(s, nz)
    core = lax.rem(m, 2)
    yh = lax.rem(lax.div(m, 2), ny)
    x = lax.div(m, 2 * ny)

    def ring(place):
        return lax.rem(place + nz, nz)

    def along(distance):
        return {"seq": yl * nz + ring(z + distance), "mp": m}

    up, down = along(1), along(-1)
    across = {"seq": (1 - yl) * nz + z, "mp": m}

    def tile(a, b, flip):
        return (lax.rem(x + a + nx, nx) * ny + lax.rem(yh + b, ny)) * 2 + (1 - core if flip else core)

    def row_device(a, b, flip):
        return {"seq": s, "mp": tile(a, b, flip)}

    sibling = row_device(0, 0, True)
    others = [(a, b) for a in range(nx) for b in range(ny) if a or b]

    barrier = pltpu.get_barrier_semaphore()
    greeted = [up, down, along(jump), along(-jump), across, sibling] + [row_device(a, b, False) for a, b in others]
    for device in greeted:
        pl.semaphore_signal(barrier, inc=1, device_id=device, device_id_type=MESH)

    def shard(row, owner):
        start = pl.multiple_of((row * nz + ring(owner)) * depth, depth)
        return wg.at[pl.ds(start, depth), :]

    own_rows = pl.ds(pl.multiple_of(s * depth, depth), depth)
    own_out = vb.at[z, pl.ds(pl.multiple_of(rows + yl * depth, depth), depth), :]
    loads = [
        pltpu.make_async_copy(wq, wg.at[own_rows, pl.ds(0, hw)], l_s.at[0]),
        pltpu.make_async_copy(wk, wg.at[own_rows, pl.ds(hw, hw)], l_s.at[1]),
        pltpu.make_async_copy(wv, wg.at[own_rows, pl.ds(2 * hw, hw)], l_s.at[2]),
        pltpu.make_async_copy(tok, xg.at[m], l_s.at[3]),
        pltpu.make_async_copy(wo, own_out, l_s.at[4]),
        pltpu.make_async_copy(gain, gv, l_s.at[5]),
        pltpu.make_async_copy(seg, sv, l_s.at[6]),
    ]
    for load in loads:
        load.start()
    mb[...] = jnp.full(mb.shape, MASKED_SCORE, jnp.float32)
    lb[...] = jnp.zeros(lb.shape, jnp.float32)
    ab[...] = jnp.zeros(ab.shape, jnp.float32)
    for load in loads:
        load.wait()
    pl.semaphore_wait(barrier, len(greeted))

    def w_send(way, offset):
        sign = 1 - 2 * way
        ref = shard(yl, z if offset in (1, jump) else z - sign * (offset - 1))
        device = along(sign * jump) if offset == jump else (up, down)[way]
        return remote(ref, ref, w_s.at[way, offset], w_r.at[way, offset], device)

    def w_arrival(way, offset):
        ref = shard(yl, z - (1 - 2 * way) * offset)
        return remote(ref, ref, w_s.at[way, offset], w_r.at[way, offset], up)

    def w_hand(way, offset):
        ref = shard(yl, z - (1 - 2 * way) * offset)
        return remote(ref, ref, wy_s.at[way, offset], wy_r.at[way, offset], across)

    def w_handed(way, offset):
        ref = shard(1 - yl, z - (1 - 2 * way) * offset)
        return remote(ref, ref, wy_s.at[way, offset], wy_r.at[way, offset], across)

    last_offset = (up_steps, down_steps)

    def w_event(offset):
        for way in (0, 1):
            if offset <= last_offset[way]:
                w_arrival(way, offset).wait_recv()
                if offset + 1 != jump and offset < last_offset[way]:
                    w_send(way, offset + 1).start()
                w_hand(way, offset).start()

    for way in (0, 1):
        w_send(way, 1).start()
    for way in (0, 1):
        w_send(way, jump).start()
    w_hand(0, 0).start()

    def tok_copy(slot, a, b, flip, device):
        index = (a * ny + b) * 2 + flip
        ref = xg.at[slot]
        return remote(ref, ref, tok_s.at[index], tok_r.at[index], device)

    def tok_arrival(a, b, flip):
        return tok_copy(tile(-a, b, flip), a, b, flip, sibling)

    tok_sends = [tok_copy(m, 0, 1, 0, row_device(0, 1, False))]
    tok_sends += [tok_copy(m, a, 0, 0, row_device(a, 0, False)) for a in range(1, nx)]
    tok_sends += [tok_copy(m, 0, 0, 1, sibling)]
    for copy in tok_sends:
        copy.start()
    out_weight = remote(own_out, own_out, o_s.at[0], o_r.at[0], across)
    out_weight.start()

    def tok_pass(a, b):
        tok_arrival(a, b, 0).wait_recv()
        later = []
        if (a, b) == (0, 1):
            later += [tok_copy(tile(0, 1, False), c, 1, 0, row_device(c, 0, False)) for c in range(1, nx)]
        later += [tok_copy(tile(-a, b, False), a, b, 1, sibling)]
        for copy in later:
            copy.start()
        tok_sends.extend(later)

    w_event(1)
    tok_pass(0, 1)
    w_event(2)
    for a in range(1, nx):
        tok_pass(a, 0)
    w_event(5)
    w_event(3)
    for a in range(1, nx):
        tok_pass(a, 1)
    w_event(6)
    w_event(4)
    w_event(7)

    for a, b in [(0, 0)] + others:
        tok_arrival(a, b, 1).wait_recv()
    square = jnp.zeros((rows, hw), jnp.float32)
    for h in range(nm):
        part = xg[h].astype(jnp.float32)
        square = square + part * part
    mean = jnp.sum(square, axis=1, keepdims=True) * (1.0 / (nm * hw))
    scale = jnp.broadcast_to(lax.rsqrt(mean + EPSILON), (rows, hw))
    for h in range(nm):
        part = xg[h].astype(jnp.float32) * scale * gv[:, h * hw:(h + 1) * hw]
        nb[:, h * hw:(h + 1) * hw] = part.astype(jnp.bfloat16)

    w_event(8)
    w_handed(0, 0).wait_recv()
    for offset in (1, 2, 5, 3, 6, 4, 7, 8):
        for way in (0, 1):
            if offset <= last_offset[way]:
                w_handed(way, offset).wait_recv()
    out_weight_in = vb.at[z, pl.ds(pl.multiple_of(rows + (1 - yl) * depth, depth), depth), :]
    remote(out_weight_in, out_weight_in, o_s.at[0], o_r.at[0], across).wait_recv()

    half = hw // 2
    middle = (rows + 2 * depth) // 2
    pieces = (
        (kt, 0, half), (kt, half, half + 16), (vb, 0, middle), (vb, middle, middle),
    )

    def kv_copy(piece, way, step, offset, device):
        buf, start, length = pieces[piece]
        ref = buf.at[ring(jnp.where(way == 0, z - offset, z + offset)), pl.ds(start, length), :]
        return remote(ref, ref, kv_s.at[piece, way], kv_r.at[piece, way, step], device)

    def kv_send(piece, way, step):
        return kv_copy(piece, way, step, step - 1, (up, down)[way])

    def kv_arrival(piece, way, step):
        return kv_copy(piece, way, step, step, (up, down)[way])

    proj = jnp.dot(nb[...], wg[:, hw:], preferred_element_type=jnp.float32)
    kt[z, :hw, :] = jnp.transpose(proj[:, :hw]).astype(jnp.bfloat16)
    kt[z, hw:hw + 16, :] = jnp.broadcast_to(sv[...].astype(jnp.float32), (16, rows)).astype(jnp.bfloat16)
    vb[z, :rows, :] = proj[:, hw:].astype(jnp.bfloat16)
    for piece in range(4):
        for way in (0, 1):
            kv_send(piece, way, 1).start()
    qb[1] = jnp.dot(nb[...], wg[:, :hw], preferred_element_type=jnp.float32).astype(jnp.bfloat16)
    query_copy = remote(qb.at[1], qb.at[0], x_s.at[0], x_r.at[0], across)

    @pl.when(yl == 1)
    def _():
        query_copy.start()

    slope = slopes[m]
    inv_scale = 1.0 / math.sqrt(hw)

    def attend(group, block):
        bias = kt[block, hw:hw + 16, :].astype(jnp.float32)[:1, :] * slope
        scores = jnp.dot(qb[group], kt[block, :hw, :], preferred_element_type=jnp.float32)
        scores = scores * inv_scale + bias
        reach = jnp.where(group == 0, nz * rows, (z - block) * rows)
        row = lax.broadcasted_iota(jnp.int32, scores.shape, 0)
        col = lax.broadcasted_iota(jnp.int32, scores.shape, 1)
        scores = jnp.where(col - row <= reach, scores, MASKED_SCORE)
        old = mb[group]
        new = jnp.maximum(old, jnp.max(scores, axis=1, keepdims=True))
        weights = jnp.exp(scores - jnp.concatenate([new] * (rows // hw), axis=1))
        factor = jnp.exp(old - new)
        total = lb[group] * factor
        for part in range(rows // hw):
            total = total + weights[:, part * hw:(part + 1) * hw]
        mb[group] = new
        lb[group] = total
        ab[group] = ab[group] * factor + jnp.dot(
            weights.astype(jnp.bfloat16), vb[block, :rows, :], preferred_element_type=jnp.float32
        )

    def kv_step(step, carry):
        def part(index, inner):
            for piece in range(4):
                for way in (0, 1):
                    @pl.when((index == piece) & (step <= last_offset[way]))
                    def _():
                        kv_arrival(piece, way, step).wait_recv()
                        kv_send(piece, way, step).wait_send()

                        @pl.when(step < last_offset[way])
                        def _():
                            kv_send(piece, way, step + 1).start()

            before = step - 1
            way, group = lax.div(index, 2), 1 - lax.rem(index, 2)
            block = ring(jnp.where(way == 0, z - before, z + before))

            @pl.when((index == 1) & (before == 0) & (yl == 0))
            def _():
                query_copy.wait_recv()

            wanted = jnp.where(group == 0, yl == 0, block <= z)
            exists = (way == 0) | ((before >= 1) & (before <= down_steps))

            @pl.when(wanted & exists)
            def _():
                attend(group, block)

            return inner

        return lax.fori_loop(0, 4, part, carry)

    lax.fori_loop(1, up_steps + 2, kv_step, 0)

    out_copy = remote(ob.at[0], ob.at[1], x_s.at[1], x_r.at[1], across)
    stat_copy = remote(sb.at[0], sb.at[1], x_s.at[2], x_r.at[2], across)

    @pl.when(yl == 0)
    def _():
        total = jnp.sum(lb[0], axis=1, keepdims=True)
        ob[0] = (ab[0] / total).astype(jnp.bfloat16)
        out_copy.start()
        level = jnp.broadcast_to(mb[0] + jnp.log(total), (rows, hw))
        sb[0] = jnp.transpose(level)[:8, :]
        stat_copy.start()

    total = jnp.sum(lb[1], axis=1, keepdims=True)
    own = ab[1] / total

    @pl.when(yl == 0)
    def _():
        att[m] = own.astype(jnp.bfloat16)

    @pl.when(yl == 1)
    def _():
        own_level = jnp.broadcast_to(mb[1] + jnp.log(total), (rows, hw))
        stat_copy.wait_recv()
        other_level = jnp.transpose(jnp.broadcast_to(sb[1][:1, :], (hw, rows)))
        share = 1.0 / (1.0 + jnp.exp(other_level - own_level))
        out_copy.wait_recv()
        merged = own * share + ob[1].astype(jnp.float32) * (1.0 - share)
        att[m] = merged.astype(jnp.bfloat16)

    def att_copy(slot, a, b, sems, device):
        ref = att.at[slot]
        return remote(ref, ref, sems[0].at[a * ny + b], sems[1].at[a * ny + b], device)

    direct, handed = (a_s, a_r), (f_s, f_r)
    att_sends = [att_copy(m, a, b, direct, row_device(a, b, False)) for a, b in reversed(others)]
    att_sends += [att_copy(m, 0, 0, handed, sibling)]
    for copy in att_sends:
        copy.start()

    for way in (0, 1):
        for offset in range(1, last_offset[way] + 1):
            w_send(way, offset).wait_send()
            w_hand(way, offset).wait_send()
    w_hand(0, 0).wait_send()
    out_weight.wait_send()
    for copy in tok_sends:
        copy.wait_send()

    @pl.when(yl == 1)
    def _():
        query_copy.wait_send()

    @pl.when(yl == 0)
    def _():
        out_copy.wait_send()
        stat_copy.wait_send()

    for a, b in others:
        att_copy(tile(-a, b, False), a, b, direct, sibling).wait_recv()
        copy = att_copy(tile(-a, b, False), a, b, handed, sibling)
        copy.start()
        att_sends.append(copy)
    for a, b in [(0, 0)] + others:
        att_copy(tile(-a, b, True), a, b, handed, sibling).wait_recv()

    mixed = xg[m].astype(jnp.float32)
    per_pair = 2 * hw // depth
    for pair in range(nm // 2):
        left = jnp.concatenate([att[2 * pair], att[2 * pair + 1]], axis=1)
        parts = []
        for owner in range(pair * per_pair, (pair + 1) * per_pair):
            start = rows + (owner // nz) * depth
            parts.append(vb[owner % nz, start:start + depth, :])
        mixed = mixed + jnp.dot(left, jnp.concatenate(parts, axis=0), preferred_element_type=jnp.float32)
    out[...] = mixed.astype(jnp.bfloat16)

    for copy in att_sends:
        copy.wait_send()


def on_device(nz, nx, ny, tokens, norm_gain, w_query, w_key, w_value, w_out, head_slope, segment_ids):
    rows, hw = tokens.shape
    depth = w_query.shape[0]
    nm = nx * ny * 2
    steps = nz // 2 + 1
    vmem = pl.BlockSpec(memory_space=pltpu.VMEM)
    hbm = pl.BlockSpec(memory_space=pltpu.HBM)
    dma = pltpu.SemaphoreType.DMA
    return pl.pallas_call(
        functools.partial(kernel, nz, nx, ny),
        out_shape=jax.ShapeDtypeStruct((rows, hw), jnp.bfloat16),
        in_specs=[hbm] * 6 + [pl.BlockSpec(memory_space=pltpu.SMEM), hbm],
        out_specs=vmem,
        scratch_shapes=[
            pltpu.VMEM((nm, rows, hw), jnp.bfloat16),
            pltpu.VMEM((rows, nm * hw), jnp.bfloat16),
            pltpu.VMEM((2 * nz * depth, 3 * hw), jnp.bfloat16),
            pltpu.VMEM((1, nm * hw), jnp.float32),
            pltpu.VMEM((1, rows), jnp.int32),
            pltpu.VMEM((nz, hw + 16, rows), jnp.bfloat16),
            pltpu.VMEM((nz, rows + 2 * depth, hw), jnp.bfloat16),
            pltpu.VMEM((2, rows, hw), jnp.bfloat16),
            pltpu.VMEM((2, rows, hw), jnp.float32),
            pltpu.VMEM((2, rows, hw), jnp.float32),
            pltpu.VMEM((2, rows, hw), jnp.float32),
            pltpu.VMEM((2, rows, hw), jnp.bfloat16),
            pltpu.VMEM((2, 8, rows), jnp.float32),
            pltpu.VMEM((nm, rows, hw), jnp.bfloat16),
            dma((7,)),
            dma((1,)), dma((1,)),
            dma((nm,)), dma((nm,)),
            dma((2, steps)), dma((2, steps)),
            dma((2, steps)), dma((2, steps)),
            dma((4, 2)), dma((4, 2, steps)),
            dma((3,)), dma((3,)),
            dma((nx * ny,)), dma((nx * ny,)),
            dma((nx * ny,)), dma((nx * ny,)),
        ],
        compiler_params=pltpu.CompilerParams(
            collective_id=0, has_side_effects=True, vmem_limit_bytes=60 << 20
        ),
        name="sublayer",
    )(
        tokens, norm_gain.reshape(1, -1), w_query, w_key, w_value, w_out, head_slope,
        segment_ids.reshape(1, -1),
    )


def solution(mesh):
    nz = mesh.shape["seq"] // 2
    ny = 2
    nx = mesh.shape["mp"] // (2 * ny)
    return jax.shard_map(
        functools.partial(on_device, nz, nx, ny),
        mesh=mesh,
        in_specs=(
            P("seq", "mp"), P(), P("seq", "mp"), P("seq", "mp"),
            P("seq", "mp"), P("seq", "mp"), P(), P("seq"),
        ),
        out_specs=P("seq", "mp"),
        check_vma=False,
    )
```

```python
import functools
import math

import jax
import jax.numpy as jnp
from jax import lax
from jax.experimental import pallas as pl
from jax.experimental.pallas import tpu as pltpu
from jax.sharding import PartitionSpec as P

EPSILON = 1e-05
MASKED_SCORE = -1e30
MESH = pl.DeviceIdType.MESH


def remote(src, dst, send, recv, device):
    return pltpu.make_async_remote_copy(
        src_ref=src, dst_ref=dst, send_sem=send, recv_sem=recv, device_id=device, device_id_type=MESH
    )


def kernel(
    nz, nx, ny, tok, gain, wq, wk, wv, wo, slopes, seg, out,
    xg, nb, wg, wog, gv, sv, kt, vb, qb, mb, lb, ab, ob, sb, att,
    l_s, o_s, o_r, p_s, p_r, h_s, h_r, tok_s, tok_r, w_s, w_r, wy_r, kv_s, kv_r, x_s, x_r, a_s, a_r, f_s, f_r,
):
    rows, hw = tok.shape
    depth = wq.shape[0]
    nm = nx * ny * 2
    up_steps = nz // 2
    down_steps = nz - 1 - up_steps
    jump = 5
    s = lax.axis_index("seq")
    m = lax.axis_index("mp")
    z = lax.rem(s, nz)
    yl = lax.div(s, nz)
    core = lax.rem(m, 2)
    yh = lax.rem(lax.div(m, 2), ny)
    x = lax.div(m, 2 * ny)

    def arrived(ref, sem):
        pltpu.make_async_copy(ref, ref, sem).wait()

    def ring(place):
        return lax.rem(place + nz, nz)

    def along(distance):
        return {"seq": yl * nz + ring(z + distance), "mp": m}

    up, down = along(1), along(-1)
    across = {"seq": (1 - yl) * nz + z, "mp": m}

    def tile(a, b, flip):
        return (lax.rem(x + a + nx, nx) * ny + lax.rem(yh + b, ny)) * 2 + (1 - core if flip else core)

    def row_device(a, b, flip):
        return {"seq": s, "mp": tile(a, b, flip)}

    sibling = row_device(0, 0, True)
    others = [(a, b) for a in range(nx) for b in range(ny) if a or b]

    barrier = pltpu.get_barrier_semaphore()
    greeted = [up, down, along(jump), along(-jump), across, sibling] + [row_device(a, b, False) for a, b in others]
    for device in greeted:
        pl.semaphore_signal(barrier, inc=1, device_id=device, device_id_type=MESH)

    def shard(row, owner):
        start = pl.multiple_of((row * nz + ring(owner)) * depth, depth)
        return wg.at[pl.ds(start, depth), :]

    own_rows = pl.ds(pl.multiple_of(s * depth, depth), depth)
    own_out = wog.at[z, yl]
    loads = [
        pltpu.make_async_copy(wq, wg.at[own_rows, pl.ds(0, hw)], l_s.at[0]),
        pltpu.make_async_copy(wk, wg.at[own_rows, pl.ds(hw, hw)], l_s.at[1]),
        pltpu.make_async_copy(wv, wg.at[own_rows, pl.ds(2 * hw, hw)], l_s.at[2]),
        pltpu.make_async_copy(tok, xg.at[m], l_s.at[3]),
        pltpu.make_async_copy(wo, own_out, l_s.at[4]),
        pltpu.make_async_copy(gain, gv, l_s.at[5]),
        pltpu.make_async_copy(seg, sv, l_s.at[6]),
    ]
    for load in loads:
        load.start()
    mb[...] = jnp.full(mb.shape, MASKED_SCORE, jnp.float32)
    lb[...] = jnp.zeros(lb.shape, jnp.float32)
    ab[...] = jnp.zeros(ab.shape, jnp.float32)
    for load in loads:
        load.wait()
    pl.semaphore_wait(barrier, len(greeted))

    def w_send(way, offset):
        sign = 1 - 2 * way
        ref = shard(yl, z if offset in (1, jump) else z - sign * (offset - 1))
        device = along(sign * jump) if offset == jump else (up, down)[way]
        return remote(ref, ref, w_s.at[0], w_r.at[way, offset], device)

    def w_arrival(way, offset):
        ref = shard(yl, z - (1 - 2 * way) * offset)
        return remote(ref, ref, w_s.at[0], w_r.at[way, offset], up)

    def w_hand(way, offset):
        ref = shard(yl, z - (1 - 2 * way) * offset)
        return remote(ref, ref, w_s.at[0], wy_r.at[0], across)

    last_offset = (up_steps, down_steps)

    def w_event(offset):
        for way in (0, 1):
            if offset <= last_offset[way]:
                w_arrival(way, offset).wait_recv()
                if offset + 1 != jump and offset < last_offset[way]:
                    w_send(way, offset + 1).start()
                w_hand(way, offset).start()

    for way in (0, 1):
        w_send(way, 1).start()
    for way in (0, 1):
        w_send(way, jump).start()
    w_hand(0, 0).start()

    def tok_copy(slot, a, b, flip, device):
        ref = xg.at[slot]
        kind = 3 if flip else 2 * b if a else 1
        return remote(ref, ref, tok_s.at[0], tok_r.at[kind], device)

    tok_sends = [tok_copy(m, 0, 1, 0, row_device(0, 1, False))]
    tok_sends += [tok_copy(m, a, 0, 0, row_device(a, 0, False)) for a in range(1, nx)]
    tok_sends += [tok_copy(m, 0, 0, 1, sibling)]
    for copy in tok_sends:
        copy.start()
    out_weight = remote(own_out, own_out, o_s.at[0], o_r.at[0], across)
    out_weight.start()

    def tok_pass(a, b):
        later = []
        if (a, b) == (0, 1):
            later += [tok_copy(tile(0, 1, False), c, 1, 0, row_device(c, 0, False)) for c in range(1, nx)]
        later += [tok_copy(tile(-a, b, False), a, b, 1, sibling)]
        for copy in later:
            copy.start()

    w_event(1)
    arrived(xg.at[0], tok_r.at[1])
    tok_pass(0, 1)
    w_event(2)
    arrived(xg.at[pl.ds(0, nx - 1)], tok_r.at[0])
    for a in range(1, nx):
        tok_pass(a, 0)
    w_event(5)
    w_event(3)
    arrived(xg.at[pl.ds(0, nx - 1)], tok_r.at[2])
    for a in range(1, nx):
        tok_pass(a, 1)
    w_event(6)
    w_event(4)
    w_event(7)

    arrived(xg.at[pl.ds(0, nx * ny)], tok_r.at[3])
    square = jnp.zeros((rows, hw), jnp.float32)
    for h in range(nm):
        part = xg[h].astype(jnp.float32)
        square = square + part * part
    mean = jnp.sum(square, axis=1, keepdims=True) * (1.0 / (nm * hw))
    scale = jnp.broadcast_to(lax.rsqrt(mean + EPSILON), (rows, hw))
    for h in range(nm):
        part = xg[h].astype(jnp.float32) * scale * gv[:, h * hw:(h + 1) * hw]
        nb[:, h * hw:(h + 1) * hw] = part.astype(jnp.bfloat16)

    w_event(8)
    arrived(wg.at[pl.ds(0, nz * depth), :], wy_r.at[0])
    other_out = wog.at[z, 1 - yl]
    remote(other_out, other_out, o_s.at[0], o_r.at[0], across).wait_recv()

    half = hw // 2
    middle = rows // 2
    pieces = (
        (kt, 0, half), (kt, half, half + 16), (vb, 0, middle), (vb, middle, middle),
    )

    def kv_copy(piece, way, step, offset, device):
        buf, start, length = pieces[piece]
        ref = buf.at[ring(z - (1 - 2 * way) * offset), pl.ds(start, length), :]
        return remote(ref, ref, kv_s.at[piece, way], kv_r.at[piece, way, step - 1], device)

    def kv_comes(way, step):
        needed = z >= step if way == 0 else ring(z + step) < down_steps
        return (step <= last_offset[way]) & ((yl == 0) | needed)

    def kv_goes(way, step):
        needed = (z >= step - 1) & (z < nz - 1) if way == 0 else ring(z + step - 1) < down_steps
        return (step <= last_offset[way]) & ((yl == 0) | needed)

    def kv_send(piece, way, step):
        return kv_copy(piece, way, step, step - 1, (up, down)[way])

    def kv_arrival(piece, way, step):
        return kv_copy(piece, way, step, step, (up, down)[way])

    proj = jnp.dot(nb[...], wg[:, hw:], preferred_element_type=jnp.float32)
    kt[z, :hw, :] = jnp.transpose(proj[:, :hw]).astype(jnp.bfloat16)
    kt[z, hw:hw + 16, :] = jnp.broadcast_to(sv[...].astype(jnp.float32), (16, rows)).astype(jnp.bfloat16)
    vb[z] = proj[:, hw:].astype(jnp.bfloat16)
    for way in (0, 1):
        @pl.when(kv_goes(way, 1))
        def _():
            for piece in range(4):
                kv_send(piece, way, 1).start()

    qb[1] = jnp.dot(nb[...], wg[:, :hw], preferred_element_type=jnp.float32).astype(jnp.bfloat16)
    query_copy = remote(qb.at[1], qb.at[0], x_s.at[0], x_r.at[0], across)

    @pl.when(yl == 1)
    def _():
        query_copy.start()

    slope = slopes[m]
    inv_scale = 1.0 / math.sqrt(hw)

    def attend(group, block):
        bias = kt[block, hw:hw + 16, :].astype(jnp.float32)[:1, :] * slope
        scores = jnp.dot(qb[group], kt[block, :hw, :], preferred_element_type=jnp.float32)
        scores = scores * inv_scale + bias
        reach = nz * rows if group == 0 else (z - block) * rows
        row = lax.broadcasted_iota(jnp.int32, scores.shape, 0)
        col = lax.broadcasted_iota(jnp.int32, scores.shape, 1)
        scores = jnp.where(col - row <= reach, scores, MASKED_SCORE)
        old = mb[group]
        new = jnp.maximum(old, jnp.max(scores, axis=1, keepdims=True))
        weights = jnp.exp(scores - jnp.concatenate([new] * (rows // hw), axis=1))
        factor = jnp.exp(old - new)
        total = lb[group] * factor
        for part in range(rows // hw):
            total = total + weights[:, part * hw:(part + 1) * hw]
        mb[group] = new
        lb[group] = total
        ab[group] = ab[group] * factor + jnp.dot(
            weights.astype(jnp.bfloat16), vb[block], preferred_element_type=jnp.float32
        )

    def wo_send(way, step):
        ref = wog.at[ring(z - (1 - 2 * way) * (step - 1))]
        return remote(ref, ref, p_s.at[way], p_r.at[way, step - 1], (up, down)[way])

    def wo_step(way, step):
        ref = wog.at[ring(z - (1 - 2 * way) * step)]
        remote(ref, ref, p_s.at[way], p_r.at[way, step - 1], up).wait_recv()
        remote(ref, ref, h_s.at[0], h_r.at[0], across).start()
        wo_send(way, step).wait_send()

        @pl.when(step < last_offset[way])
        def _():
            wo_send(way, step + 1).start()

    @pl.when(yl == 1)
    def _():
        wo_send(0, 1).start()
        wo_send(1, 1).start()

    def kv_step(step, carry):
        before = step - 1
        comes = [kv_comes(way, step) for way in (0, 1)]
        went = [kv_goes(way, step) for way in (0, 1)]
        goes = [kv_goes(way, step + 1) for way in (0, 1)]
        for index in range(4):
            for way in (0, 1):
                @pl.when(comes[way])
                def _():
                    kv_arrival(index, way, step).wait_recv()

                @pl.when(went[way])
                def _():
                    kv_send(index, way, step).wait_send()

                @pl.when(goes[way])
                def _():
                    kv_send(index, way, step + 1).start()

            way, group = index // 2, 1 - index % 2
            block = ring(z - (1 - 2 * way) * before)
            if index == 1:
                @pl.when((before == 0) & (yl == 0))
                def _():
                    query_copy.wait_recv()

            wanted = yl == 0 if group == 0 else block <= z
            if way == 1:
                wanted = wanted & (before >= 1) & (before <= down_steps)

            @pl.when(wanted)
            def _():
                attend(group, block)

        for way in (0, 1):
            @pl.when((yl == 1) & (step <= last_offset[way]))
            def _():
                wo_step(way, step)

        return carry

    lax.fori_loop(1, up_steps + 2, kv_step, 0)

    out_copy = remote(ob.at[0], ob.at[1], x_s.at[1], x_r.at[1], across)
    stat_copy = remote(sb.at[0], sb.at[1], x_s.at[2], x_r.at[2], across)

    @pl.when(yl == 0)
    def _():
        total = jnp.sum(lb[0], axis=1, keepdims=True)
        ob[0] = (ab[0] / total).astype(jnp.bfloat16)
        out_copy.start()
        level = jnp.broadcast_to(mb[0] + jnp.log(total), (rows, hw))
        sb[0] = jnp.transpose(level)[:8, :]
        stat_copy.start()

    total = jnp.sum(lb[1], axis=1, keepdims=True)
    own = ab[1] / total

    @pl.when(yl == 0)
    def _():
        att[m] = own.astype(jnp.bfloat16)

    @pl.when(yl == 1)
    def _():
        own_level = jnp.broadcast_to(mb[1] + jnp.log(total), (rows, hw))
        stat_copy.wait_recv()
        other_level = jnp.transpose(jnp.broadcast_to(sb[1][:1, :], (hw, rows)))
        share = 1.0 / (1.0 + jnp.exp(other_level - own_level))
        out_copy.wait_recv()
        merged = own * share + ob[1].astype(jnp.float32) * (1.0 - share)
        att[m] = merged.astype(jnp.bfloat16)

    def att_copy(slot, a, b, sems, device):
        ref = att.at[slot]
        return remote(ref, ref, sems[0].at[0], sems[1].at[a * ny + b if sems is direct else 0], device)

    direct, handed = (a_s, a_r), (f_s, f_r)
    att_sends = [att_copy(m, a, b, direct, row_device(a, b, False)) for a, b in reversed(others)]
    att_sends += [att_copy(m, 0, 0, handed, sibling)]
    for copy in att_sends:
        copy.start()

    arrived(wg.at[pl.ds(0, (2 * nz - 1) * depth), :], w_s.at[0])
    arrived(xg.at[pl.ds(0, nm - 1)], tok_s.at[0])
    out_weight.wait_send()

    @pl.when(yl == 1)
    def _():
        arrived(wog.at[pl.ds(0, nz - 1)], h_s.at[0])

    @pl.when(yl == 0)
    def _():
        arrived(wog.at[pl.ds(0, nz - 1)], h_r.at[0])

    @pl.when(yl == 1)
    def _():
        query_copy.wait_send()

    @pl.when(yl == 0)
    def _():
        out_copy.wait_send()
        stat_copy.wait_send()

    per_head = hw // depth

    def project(head):
        first = head * per_head
        weight = wog[pl.ds(lax.rem(first, nz), per_head), lax.div(first, nz)].reshape(hw, hw)
        return jnp.dot(att[head], weight, preferred_element_type=jnp.float32)

    mixed = xg[m].astype(jnp.float32) + project(m)
    for a, b in others:
        head = tile(-a, b, False)
        att_copy(head, a, b, direct, sibling).wait_recv()
        att_copy(head, a, b, handed, sibling).start()
        mixed = mixed + project(head)
    arrived(att.at[pl.ds(0, nx * ny)], f_r.at[0])
    for a, b in [(0, 0)] + others:
        mixed = mixed + project(tile(-a, b, True))
    out[...] = mixed.astype(jnp.bfloat16)

    arrived(att.at[pl.ds(0, nx * ny - 1)], a_s.at[0])
    arrived(att.at[pl.ds(0, nx * ny)], f_s.at[0])


def on_device(nz, nx, ny, tokens, norm_gain, w_query, w_key, w_value, w_out, head_slope, segment_ids):
    rows, hw = tokens.shape
    depth = w_query.shape[0]
    nm = nx * ny * 2
    steps = nz // 2 + 1
    vmem = pl.BlockSpec(memory_space=pltpu.VMEM)
    hbm = pl.BlockSpec(memory_space=pltpu.HBM)
    dma = pltpu.SemaphoreType.DMA
    return pl.pallas_call(
        functools.partial(kernel, nz, nx, ny),
        out_shape=jax.ShapeDtypeStruct((rows, hw), jnp.bfloat16),
        in_specs=[hbm] * 6 + [pl.BlockSpec(memory_space=pltpu.SMEM), hbm],
        out_specs=vmem,
        scratch_shapes=[
            pltpu.VMEM((nm, rows, hw), jnp.bfloat16),
            pltpu.VMEM((rows, nm * hw), jnp.bfloat16),
            pltpu.VMEM((2 * nz * depth, 3 * hw), jnp.bfloat16),
            pltpu.VMEM((nz, 2, depth, hw), jnp.bfloat16),
            pltpu.VMEM((1, nm * hw), jnp.float32),
            pltpu.VMEM((1, rows), jnp.int32),
            pltpu.VMEM((nz, hw + 16, rows), jnp.bfloat16),
            pltpu.VMEM((nz, rows, hw), jnp.bfloat16),
            pltpu.VMEM((2, rows, hw), jnp.bfloat16),
            pltpu.VMEM((2, rows, hw), jnp.float32),
            pltpu.VMEM((2, rows, hw), jnp.float32),
            pltpu.VMEM((2, rows, hw), jnp.float32),
            pltpu.VMEM((2, rows, hw), jnp.bfloat16),
            pltpu.VMEM((2, 8, rows), jnp.float32),
            pltpu.VMEM((nm, rows, hw), jnp.bfloat16),
            dma((7,)),
            dma((1,)), dma((1,)),
            dma((2,)), dma((2, steps - 1)),
            dma((1,)), dma((1,)),
            dma((1,)), dma((4,)),
            dma((1,)), dma((2, steps)),
            dma((1,)),
            dma((4, 2)), dma((4, 2, steps - 1)),
            dma((3,)), dma((3,)),
            dma((1,)), dma((nx * ny,)),
            dma((1,)), dma((1,)),
        ],
        compiler_params=pltpu.CompilerParams(
            collective_id=0, has_side_effects=True, vmem_limit_bytes=60 << 20
        ),
        name="sublayer",
    )(
        tokens, norm_gain.reshape(1, -1), w_query, w_key, w_value, w_out, head_slope,
        segment_ids.reshape(1, -1),
    )


def solution(mesh):
    nz = mesh.shape["seq"] // 2
    ny = 2
    nx = mesh.shape["mp"] // (2 * ny)
    return jax.shard_map(
        functools.partial(on_device, nz, nx, ny),
        mesh=mesh,
        in_specs=(
            P("seq", "mp"), P(), P("seq", "mp"), P("seq", "mp"),
            P("seq", "mp"), P("seq", "mp"), P(), P("seq"),
        ),
        out_specs=P("seq", "mp"),
        check_vma=False,
    )
```

```python
import functools
import math

import jax
import jax.numpy as jnp
from jax import lax
from jax.experimental import pallas as pl
from jax.experimental.pallas import tpu as pltpu
from jax.sharding import PartitionSpec as P

EPSILON = 1e-05
MASKED_SCORE = -1e30
MESH = pl.DeviceIdType.MESH


def remote(src, dst, send, recv, device):
    return pltpu.make_async_remote_copy(
        src_ref=src, dst_ref=dst, send_sem=send, recv_sem=recv, device_id=device, device_id_type=MESH
    )


def kernel(
    nz, nx, ny, tok, gain, wq, wk, wv, wo, slopes, seg, out,
    xg, nb, wg, wgq, wog, gv, sv, kt, vb, qb, mb, lb, ab, ob, sb, att,
    l_s, o_s, o_r, p_s, p_r, h_s, h_r, tok_s, tok_r, w_s, w_r, wy_r, q_s, q_r, qy_r, kv_s, kv_r, x_s, x_r, a_s, a_r, f_s, f_r,
):
    rows, hw = tok.shape
    depth = wq.shape[0]
    nm = nx * ny * 2
    up_steps = nz // 2
    down_steps = nz - 1 - up_steps
    stride = 2
    s = lax.axis_index("seq")
    m = lax.axis_index("mp")
    z = lax.rem(s, nz)
    yl = lax.div(s, nz)
    core = lax.rem(m, 2)
    yh = lax.rem(lax.div(m, 2), ny)
    x = lax.div(m, 2 * ny)

    def arrived(ref, sem):
        pltpu.make_async_copy(ref, ref, sem).wait()

    def ring(place):
        return lax.rem(place + nz, nz)

    def along(distance):
        return {"seq": yl * nz + ring(z + distance), "mp": m}

    up, down = along(1), along(-1)
    across = {"seq": (1 - yl) * nz + z, "mp": m}

    def tile(a, b, flip):
        return (lax.rem(x + a + nx, nx) * ny + lax.rem(yh + b, ny)) * 2 + (1 - core if flip else core)

    def row_device(a, b, flip):
        return {"seq": s, "mp": tile(a, b, flip)}

    sibling = row_device(0, 0, True)
    others = [(a, b) for a in range(nx) for b in range(ny) if a or b]

    barrier = pltpu.get_barrier_semaphore()
    greeted = [along(way * far) for far in range(1, stride + 1) for way in (1, -1)] + [across, sibling] + [row_device(a, b, False) for a, b in others]
    for device in greeted:
        pl.semaphore_signal(barrier, inc=1, device_id=device, device_id_type=MESH)

    def shard(buf, row, owner):
        start = pl.multiple_of((row * nz + ring(owner)) * depth, depth)
        return buf.at[pl.ds(start, depth), :]

    own_rows = pl.ds(pl.multiple_of(s * depth, depth), depth)
    own_out = wog.at[z, yl]
    loads = [
        pltpu.make_async_copy(wq, wgq.at[own_rows, :], l_s.at[0]),
        pltpu.make_async_copy(wk, wg.at[own_rows, pl.ds(0, hw)], l_s.at[1]),
        pltpu.make_async_copy(wv, wg.at[own_rows, pl.ds(hw, hw)], l_s.at[2]),
        pltpu.make_async_copy(tok, xg.at[m], l_s.at[3]),
        pltpu.make_async_copy(wo, own_out, l_s.at[4]),
        pltpu.make_async_copy(gain, gv, l_s.at[5]),
        pltpu.make_async_copy(seg, sv, l_s.at[6]),
    ]
    for load in loads:
        load.start()
    mb[...] = jnp.full(mb.shape, MASKED_SCORE, jnp.float32)
    lb[...] = jnp.zeros(lb.shape, jnp.float32)
    ab[...] = jnp.zeros(ab.shape, jnp.float32)
    for load in loads:
        load.wait()
    pl.semaphore_wait(barrier, len(greeted))

    key_value, queries = (wg, w_s, w_r, wy_r), (wgq, q_s, q_r, qy_r)

    def w_send(side, way, offset):
        buf, sent, came, _ = side
        sign = 1 - 2 * way
        hops = min(offset, stride)
        ref = shard(buf, yl, z - sign * (offset - hops))
        return remote(ref, ref, sent.at[0], came.at[way, offset], along(sign * hops))

    def w_hand(side, way, offset):
        buf, sent, _, handed = side
        ref = shard(buf, yl, z - (1 - 2 * way) * offset)
        return remote(ref, ref, sent.at[0], handed.at[0], across)

    def w_event(offset, sides=None):
        for side in sides or (key_value, queries):
            for way in (0, 1):
                if offset <= last_offset[way]:
                    arrived(shard(side[0], yl, z - (1 - 2 * way) * offset), side[2].at[way, offset])
                    if offset + stride <= last_offset[way]:
                        w_send(side, way, offset + stride).start()
                    w_hand(side, way, offset).start()

    last_offset = (up_steps, down_steps)
    for first in range(1, stride + 1):
        for side in (key_value, queries):
            for way in (0, 1):
                w_send(side, way, first).start()
    for side in (key_value, queries):
        w_hand(side, 0, 0).start()

    def tok_copy(slot, a, b, flip, device):
        ref = xg.at[slot]
        kind = 3 if flip else 2 * b if a else 1
        return remote(ref, ref, tok_s.at[0], tok_r.at[kind], device)

    tok_sends = [tok_copy(m, 0, 1, 0, row_device(0, 1, False))]
    tok_sends += [tok_copy(m, a, 0, 0, row_device(a, 0, False)) for a in range(1, nx)]
    tok_sends += [tok_copy(m, 0, 0, 1, sibling)]
    for copy in tok_sends:
        copy.start()
    out_weight = remote(own_out, own_out, o_s.at[0], o_r.at[0], across)
    out_weight.start()

    def tok_pass(a, b):
        later = []
        if (a, b) == (0, 1):
            later += [tok_copy(tile(0, 1, False), c, 1, 0, row_device(c, 0, False)) for c in range(1, nx)]
        later += [tok_copy(tile(-a, b, False), a, b, 1, sibling)]
        for copy in later:
            copy.start()

    w_event(1, (key_value,))
    w_event(2, (key_value,))
    arrived(xg.at[0], tok_r.at[1])
    tok_pass(0, 1)
    arrived(xg.at[pl.ds(0, nx - 1)], tok_r.at[0])
    for a in range(1, nx):
        tok_pass(a, 0)
    w_event(1, (queries,))
    w_event(2, (queries,))
    w_event(3, (key_value,))
    w_event(4, (key_value,))
    arrived(xg.at[pl.ds(0, nx - 1)], tok_r.at[2])
    for a in range(1, nx):
        tok_pass(a, 1)
    w_event(3, (queries,))
    w_event(4, (queries,))
    w_event(5, (key_value,))
    w_event(6, (key_value,))
    arrived(xg.at[pl.ds(0, nx * ny)], tok_r.at[3])
    square = jnp.zeros((rows, hw), jnp.float32)
    for h in range(nm):
        part = xg[h].astype(jnp.float32)
        square = square + part * part
    mean = jnp.sum(square, axis=1, keepdims=True) * (1.0 / (nm * hw))
    scale = jnp.broadcast_to(lax.rsqrt(mean + EPSILON), (rows, hw))
    for h in range(nm):
        part = xg[h].astype(jnp.float32) * scale * gv[:, h * hw:(h + 1) * hw]
        nb[:, h * hw:(h + 1) * hw] = part.astype(jnp.bfloat16)

    w_event(5, (queries,))
    w_event(6, (queries,))
    w_event(7, (key_value,))
    w_event(8, (key_value,))
    w_event(7, (queries,))
    w_event(8, (queries,))
    arrived(wg.at[pl.ds(0, nz * depth), :], wy_r.at[0])

    half = hw // 2
    middle = rows // 2
    pieces = (
        (kt, 0, half), (kt, half, half + 16), (vb, 0, middle), (vb, middle, middle),
    )

    def kv_copy(piece, way, step, offset, device):
        buf, start, length = pieces[piece]
        ref = buf.at[ring(z - (1 - 2 * way) * offset), pl.ds(start, length), :]
        return remote(ref, ref, kv_s.at[piece, way], kv_r.at[piece, way, step - 1], device)

    def kv_comes(way, step):
        needed = z >= step if way == 0 else ring(z + step) < down_steps
        return (step <= last_offset[way]) & ((yl == 0) | needed)

    def kv_goes(way, step):
        needed = (z >= step - 1) & (z < nz - 1) if way == 0 else ring(z + step - 1) < down_steps
        return (step <= last_offset[way]) & ((yl == 0) | needed)

    def kv_send(piece, way, step):
        return kv_copy(piece, way, step, step - 1, (up, down)[way])

    def kv_arrival(piece, way, step):
        return kv_copy(piece, way, step, step, (up, down)[way])

    proj = jnp.dot(nb[...], wg[...], preferred_element_type=jnp.float32)
    kt[z, :hw, :] = jnp.transpose(proj[:, :hw]).astype(jnp.bfloat16)
    kt[z, hw:hw + 16, :] = jnp.broadcast_to(sv[...].astype(jnp.float32), (16, rows)).astype(jnp.bfloat16)
    vb[z] = proj[:, hw:].astype(jnp.bfloat16)
    for way in (0, 1):
        @pl.when(kv_goes(way, 1))
        def _():
            for piece in range(4):
                kv_send(piece, way, 1).start()

    arrived(wgq.at[pl.ds(0, nz * depth), :], qy_r.at[0])
    qb[1] = jnp.dot(nb[...], wgq[...], preferred_element_type=jnp.float32).astype(jnp.bfloat16)
    query_copy = remote(qb.at[1], qb.at[0], x_s.at[0], x_r.at[0], across)

    @pl.when(yl == 1)
    def _():
        query_copy.start()

    slope = slopes[m]
    inv_scale = 1.0 / math.sqrt(hw)

    def attend(group, block):
        bias = kt[block, hw:hw + 16, :].astype(jnp.float32)[:1, :] * slope
        scores = jnp.dot(qb[group], kt[block, :hw, :], preferred_element_type=jnp.float32)
        scores = scores * inv_scale + bias
        reach = nz * rows if group == 0 else (z - block) * rows
        row = lax.broadcasted_iota(jnp.int32, scores.shape, 0)
        col = lax.broadcasted_iota(jnp.int32, scores.shape, 1)
        scores = jnp.where(col - row <= reach, scores, MASKED_SCORE)
        old = mb[group]
        new = jnp.maximum(old, jnp.max(scores, axis=1, keepdims=True))
        weights = jnp.exp(scores - jnp.concatenate([new] * (rows // hw), axis=1))
        factor = jnp.exp(old - new)
        total = lb[group] * factor
        for part in range(rows // hw):
            total = total + weights[:, part * hw:(part + 1) * hw]
        mb[group] = new
        lb[group] = total
        ab[group] = ab[group] * factor + jnp.dot(
            weights.astype(jnp.bfloat16), vb[block], preferred_element_type=jnp.float32
        )

    def wo_send(way, step):
        ref = wog.at[ring(z - (1 - 2 * way) * (step - 1))]
        return remote(ref, ref, p_s.at[way], p_r.at[way, step - 1], (up, down)[way])

    def wo_step(way, step):
        ref = wog.at[ring(z - (1 - 2 * way) * step)]
        remote(ref, ref, p_s.at[way], p_r.at[way, step - 1], up).wait_recv()
        remote(ref, ref, h_s.at[0], h_r.at[0], across).start()
        wo_send(way, step).wait_send()

        @pl.when(step < last_offset[way])
        def _():
            wo_send(way, step + 1).start()

    other_out = wog.at[z, 1 - yl]
    remote(other_out, other_out, o_s.at[0], o_r.at[0], across).wait_recv()

    @pl.when(yl == 1)
    def _():
        wo_send(0, 1).start()
        wo_send(1, 1).start()

    def kv_step(step, carry):
        before = step - 1
        comes = [kv_comes(way, step) for way in (0, 1)]
        went = [kv_goes(way, step) for way in (0, 1)]
        goes = [kv_goes(way, step + 1) for way in (0, 1)]
        for index in range(4):
            for way in (0, 1):
                @pl.when(comes[way])
                def _():
                    kv_arrival(index, way, step).wait_recv()

                @pl.when(went[way])
                def _():
                    kv_send(index, way, step).wait_send()

                @pl.when(goes[way])
                def _():
                    kv_send(index, way, step + 1).start()

            way, group = index // 2, 1 - index % 2
            block = ring(z - (1 - 2 * way) * before)
            if index == 1:
                @pl.when((before == 0) & (yl == 0))
                def _():
                    query_copy.wait_recv()

            wanted = yl == 0 if group == 0 else block <= z
            if way == 1:
                wanted = wanted & (before >= 1) & (before <= down_steps)

            @pl.when(wanted)
            def _():
                attend(group, block)

        for way in (0, 1):
            @pl.when((yl == 1) & (step <= last_offset[way]))
            def _():
                wo_step(way, step)

        return carry

    lax.fori_loop(1, up_steps + 2, kv_step, 0)

    out_copy = remote(ob.at[0], ob.at[1], x_s.at[1], x_r.at[1], across)
    stat_copy = remote(sb.at[0], sb.at[1], x_s.at[2], x_r.at[2], across)

    @pl.when(yl == 0)
    def _():
        total = jnp.sum(lb[0], axis=1, keepdims=True)
        ob[0] = (ab[0] / total).astype(jnp.bfloat16)
        out_copy.start()
        level = jnp.broadcast_to(mb[0] + jnp.log(total), (rows, hw))
        sb[0] = jnp.transpose(level)[:8, :]
        stat_copy.start()

    total = jnp.sum(lb[1], axis=1, keepdims=True)
    own = ab[1] / total

    @pl.when(yl == 0)
    def _():
        att[m] = own.astype(jnp.bfloat16)

    @pl.when(yl == 1)
    def _():
        own_level = jnp.broadcast_to(mb[1] + jnp.log(total), (rows, hw))
        stat_copy.wait_recv()
        other_level = jnp.transpose(jnp.broadcast_to(sb[1][:1, :], (hw, rows)))
        share = 1.0 / (1.0 + jnp.exp(other_level - own_level))
        out_copy.wait_recv()
        merged = own * share + ob[1].astype(jnp.float32) * (1.0 - share)
        att[m] = merged.astype(jnp.bfloat16)

    def att_copy(slot, a, b, sems, device):
        ref = att.at[slot]
        return remote(ref, ref, sems[0].at[0], sems[1].at[a * ny + b if sems is direct else 0], device)

    direct, handed = (a_s, a_r), (f_s, f_r)
    att_sends = [att_copy(m, a, b, direct, row_device(a, b, False)) for a, b in [(1, 0), (3, 0), (0, 1), (2, 0), (1, 1), (3, 1), (2, 1)]]
    att_sends += [att_copy(m, 0, 0, handed, sibling)]
    for copy in att_sends:
        copy.start()

    arrived(wg.at[pl.ds(0, (2 * nz - 1) * depth), :], w_s.at[0])
    arrived(wgq.at[pl.ds(0, (2 * nz - 1) * depth), :], q_s.at[0])
    arrived(xg.at[pl.ds(0, nm - 1)], tok_s.at[0])
    out_weight.wait_send()

    @pl.when(yl == 1)
    def _():
        arrived(wog.at[pl.ds(0, nz - 1)], h_s.at[0])

    @pl.when(yl == 0)
    def _():
        arrived(wog.at[pl.ds(0, nz - 1)], h_r.at[0])

    @pl.when(yl == 1)
    def _():
        query_copy.wait_send()

    @pl.when(yl == 0)
    def _():
        out_copy.wait_send()
        stat_copy.wait_send()

    per_head = hw // depth

    def project(head):
        first = head * per_head
        weight = wog[pl.ds(lax.rem(first, nz), per_head), lax.div(first, nz)].reshape(hw, hw)
        return jnp.dot(att[head], weight, preferred_element_type=jnp.float32)

    mixed = xg[m].astype(jnp.float32) + project(m)
    for a, b in [(1, 0), (3, 0), (0, 1), (2, 0), (1, 1), (3, 1), (2, 1)]:
        head = tile(-a, b, False)
        att_copy(head, a, b, direct, sibling).wait_recv()
        att_copy(head, a, b, handed, sibling).start()
        mixed = mixed + project(head)
    arrived(att.at[pl.ds(0, nx * ny)], f_r.at[0])
    for a, b in [(0, 0)] + others:
        mixed = mixed + project(tile(-a, b, True))
    out[...] = mixed.astype(jnp.bfloat16)

    arrived(att.at[pl.ds(0, nx * ny - 1)], a_s.at[0])
    arrived(att.at[pl.ds(0, nx * ny)], f_s.at[0])


def on_device(nz, nx, ny, tokens, norm_gain, w_query, w_key, w_value, w_out, head_slope, segment_ids):
    rows, hw = tokens.shape
    depth = w_query.shape[0]
    nm = nx * ny * 2
    steps = nz // 2 + 1
    vmem = pl.BlockSpec(memory_space=pltpu.VMEM)
    hbm = pl.BlockSpec(memory_space=pltpu.HBM)
    dma = pltpu.SemaphoreType.DMA
    return pl.pallas_call(
        functools.partial(kernel, nz, nx, ny),
        out_shape=jax.ShapeDtypeStruct((rows, hw), jnp.bfloat16),
        in_specs=[hbm] * 6 + [pl.BlockSpec(memory_space=pltpu.SMEM), hbm],
        out_specs=vmem,
        scratch_shapes=[
            pltpu.VMEM((nm, rows, hw), jnp.bfloat16),
            pltpu.VMEM((rows, nm * hw), jnp.bfloat16),
            pltpu.VMEM((2 * nz * depth, 2 * hw), jnp.bfloat16),
            pltpu.VMEM((2 * nz * depth, hw), jnp.bfloat16),
            pltpu.VMEM((nz, 2, depth, hw), jnp.bfloat16),
            pltpu.VMEM((1, nm * hw), jnp.float32),
            pltpu.VMEM((1, rows), jnp.int32),
            pltpu.VMEM((nz, hw + 16, rows), jnp.bfloat16),
            pltpu.VMEM((nz, rows, hw), jnp.bfloat16),
            pltpu.VMEM((2, rows, hw), jnp.bfloat16),
            pltpu.VMEM((2, rows, hw), jnp.float32),
            pltpu.VMEM((2, rows, hw), jnp.float32),
            pltpu.VMEM((2, rows, hw), jnp.float32),
            pltpu.VMEM((2, rows, hw), jnp.bfloat16),
            pltpu.VMEM((2, 8, rows), jnp.float32),
            pltpu.VMEM((nm, rows, hw), jnp.bfloat16),
            dma((7,)),
            dma((1,)), dma((1,)),
            dma((2,)), dma((2, steps - 1)),
            dma((1,)), dma((1,)),
            dma((1,)), dma((4,)),
            dma((1,)), dma((2, steps)),
            dma((1,)),
            dma((1,)), dma((2, steps)),
            dma((1,)),
            dma((4, 2)), dma((4, 2, steps - 1)),
            dma((3,)), dma((3,)),
            dma((1,)), dma((nx * ny,)),
            dma((1,)), dma((1,)),
        ],
        compiler_params=pltpu.CompilerParams(
            collective_id=0, has_side_effects=True, vmem_limit_bytes=60 << 20
        ),
        name="sublayer",
    )(
        tokens, norm_gain.reshape(1, -1), w_query, w_key, w_value, w_out, head_slope,
        segment_ids.reshape(1, -1),
    )


def solution(mesh):
    nz = mesh.shape["seq"] // 2
    ny = 2
    nx = mesh.shape["mp"] // (2 * ny)
    return jax.shard_map(
        functools.partial(on_device, nz, nx, ny),
        mesh=mesh,
        in_specs=(
            P("seq", "mp"), P(), P("seq", "mp"), P("seq", "mp"),
            P("seq", "mp"), P("seq", "mp"), P(), P("seq"),
        ),
        out_specs=P("seq", "mp"),
        check_vma=False,
    )
```

```python
import functools
import math

import jax
import jax.numpy as jnp
from jax import lax
from jax.experimental import pallas as pl
from jax.experimental.pallas import tpu as pltpu
from jax.sharding import PartitionSpec as P

EPSILON = 1e-05
MASKED_SCORE = -1e30
MESH = pl.DeviceIdType.MESH


def remote(src, dst, send, recv, device):
    return pltpu.make_async_remote_copy(
        src_ref=src, dst_ref=dst, send_sem=send, recv_sem=recv, device_id=device, device_id_type=MESH
    )


def kernel(
    nz, nx, ny, tok, gain, wq, wk, wv, wo, slopes, seg, out,
    xg, nb, wg, wgq, wog, gv, sv, kt, vb, qb, mb, lb, ab, ob, sb, att,
    l_s, o_s, o_r, p_s, p_r, h_s, h_r, tok_s, tok_r, w_s, w_r, wy_r, q_s, q_r, qy_r, kv_s, kv_r, x_s, x_r, a_s, a_r, f_s, f_r,
):
    rows, hw = tok.shape
    depth = wq.shape[0]
    nm = nx * ny * 2
    up_steps = nz // 2
    down_steps = nz - 1 - up_steps
    origin = {1: 0, 2: 0, 3: 2, 4: 2, 5: 4, 6: 4, 7: 6, 8: 6}
    hops = sorted(set(offset - origin[offset] for offset in origin))
    s = lax.axis_index("seq")
    m = lax.axis_index("mp")
    z = lax.rem(s, nz)
    yl = lax.div(s, nz)
    core = lax.rem(m, 2)
    yh = lax.rem(lax.div(m, 2), ny)
    x = lax.div(m, 2 * ny)

    def arrived(ref, sem):
        pltpu.make_async_copy(ref, ref, sem).wait()

    def ring(place):
        return lax.rem(place + nz, nz)

    def along(distance):
        return {"seq": yl * nz + ring(z + distance), "mp": m}

    up, down = along(1), along(-1)
    across = {"seq": (1 - yl) * nz + z, "mp": m}

    def tile(a, b, flip):
        return (lax.rem(x + a + nx, nx) * ny + lax.rem(yh + b, ny)) * 2 + (1 - core if flip else core)

    def row_device(a, b, flip):
        return {"seq": s, "mp": tile(a, b, flip)}

    sibling = row_device(0, 0, True)
    others = [(a, b) for a in range(nx) for b in range(ny) if a or b]

    barrier = pltpu.get_barrier_semaphore()
    greeted = [along(way * far) for far in hops for way in (1, -1)] + [across, sibling] + [row_device(a, b, False) for a, b in others]
    for device in greeted:
        pl.semaphore_signal(barrier, inc=1, device_id=device, device_id_type=MESH)

    def shard(buf, row, owner):
        start = pl.multiple_of((row * nz + ring(owner)) * depth, depth)
        return buf.at[pl.ds(start, depth), :]

    own_rows = pl.ds(pl.multiple_of(s * depth, depth), depth)
    own_out = wog.at[z, yl]
    loads = [
        pltpu.make_async_copy(wq, wgq.at[own_rows, :], l_s.at[0]),
        pltpu.make_async_copy(wk, wg.at[own_rows, pl.ds(0, hw)], l_s.at[1]),
        pltpu.make_async_copy(wv, wg.at[own_rows, pl.ds(hw, hw)], l_s.at[2]),
        pltpu.make_async_copy(tok, xg.at[m], l_s.at[3]),
        pltpu.make_async_copy(wo, own_out, l_s.at[4]),
        pltpu.make_async_copy(gain, gv, l_s.at[5]),
        pltpu.make_async_copy(seg, sv, l_s.at[6]),
    ]
    for load in loads:
        load.start()
    mb[...] = jnp.full(mb.shape, MASKED_SCORE, jnp.float32)
    lb[...] = jnp.zeros(lb.shape, jnp.float32)
    ab[...] = jnp.zeros(ab.shape, jnp.float32)
    for load in loads:
        load.wait()
    pl.semaphore_wait(barrier, len(greeted))

    key_value, queries = (wg, w_s, w_r, wy_r), (wgq, q_s, q_r, qy_r)

    def w_send(side, way, offset):
        buf, sent, came, _ = side
        sign = 1 - 2 * way
        ref = shard(buf, yl, z - sign * origin[offset])
        return remote(ref, ref, sent.at[0], came.at[way, offset], along(sign * (offset - origin[offset])))

    def w_hand(side, way, offset):
        buf, sent, _, handed = side
        ref = shard(buf, yl, z - (1 - 2 * way) * offset)
        return remote(ref, ref, sent.at[0], handed.at[0], across)

    def w_event(offset, sides=None):
        for side in sides or (key_value, queries):
            for way in (0, 1):
                if offset <= last_offset[way]:
                    arrived(shard(side[0], yl, z - (1 - 2 * way) * offset), side[2].at[way, offset])
                    for later in range(last_offset[way], offset, -1):
                        if origin[later] == offset:
                            w_send(side, way, later).start()
                    w_hand(side, way, offset).start()

    last_offset = (up_steps, down_steps)
    for first in range(1, up_steps + 1):
        if origin[first] == 0:
            for side in (key_value, queries):
                for way in (0, 1):
                    w_send(side, way, first).start()
    for side in (key_value, queries):
        w_hand(side, 0, 0).start()

    def tok_copy(slot, a, b, flip, device):
        ref = xg.at[slot]
        kind = 3 if flip else 2 * b if a else 1
        return remote(ref, ref, tok_s.at[0], tok_r.at[kind], device)

    tok_sends = [tok_copy(m, 0, 1, 0, row_device(0, 1, False))]
    tok_sends += [tok_copy(m, a, 0, 0, row_device(a, 0, False)) for a in range(1, nx)]
    tok_sends += [tok_copy(m, 0, 0, 1, sibling)]
    for copy in tok_sends:
        copy.start()
    out_weight = remote(own_out, own_out, o_s.at[0], o_r.at[0], across)
    out_weight.start()

    def tok_pass(a, b):
        later = []
        if (a, b) == (0, 1):
            later += [tok_copy(tile(0, 1, False), c, 1, 0, row_device(c, 0, False)) for c in range(1, nx)]
        later += [tok_copy(tile(-a, b, False), a, b, 1, sibling)]
        for copy in later:
            copy.start()

    w_event(1, (key_value,))
    w_event(2, (key_value,))
    arrived(xg.at[0], tok_r.at[1])
    tok_pass(0, 1)
    arrived(xg.at[pl.ds(0, nx - 1)], tok_r.at[0])
    for a in range(1, nx):
        tok_pass(a, 0)
    w_event(1, (queries,))
    w_event(2, (queries,))
    w_event(3, (key_value,))
    w_event(4, (key_value,))
    arrived(xg.at[pl.ds(0, nx - 1)], tok_r.at[2])
    for a in range(1, nx):
        tok_pass(a, 1)
    w_event(3, (queries,))
    w_event(4, (queries,))
    w_event(5, (key_value,))
    w_event(6, (key_value,))
    arrived(xg.at[pl.ds(0, nx * ny)], tok_r.at[3])
    square = jnp.zeros((rows, hw), jnp.float32)
    for h in range(nm):
        part = xg[h].astype(jnp.float32)
        square = square + part * part
    mean = jnp.sum(square, axis=1, keepdims=True) * (1.0 / (nm * hw))
    scale = jnp.broadcast_to(lax.rsqrt(mean + EPSILON), (rows, hw))
    for h in range(nm):
        part = xg[h].astype(jnp.float32) * scale * gv[:, h * hw:(h + 1) * hw]
        nb[:, h * hw:(h + 1) * hw] = part.astype(jnp.bfloat16)

    w_event(5, (queries,))
    w_event(6, (queries,))
    w_event(7, (key_value,))
    w_event(8, (key_value,))
    w_event(7, (queries,))
    w_event(8, (queries,))
    arrived(wg.at[pl.ds(0, nz * depth), :], wy_r.at[0])

    half = hw // 2
    middle = rows // 2
    pieces = (
        (kt, 0, half), (kt, half, half + 16), (vb, 0, middle), (vb, middle, middle),
    )

    def kv_copy(piece, way, step, offset, device):
        buf, start, length = pieces[piece]
        ref = buf.at[ring(z - (1 - 2 * way) * offset), pl.ds(start, length), :]
        return remote(ref, ref, kv_s.at[piece, way], kv_r.at[piece, way, step - 1], device)

    def kv_comes(way, step):
        needed = z >= step if way == 0 else ring(z + step) < down_steps
        return (step <= last_offset[way]) & ((yl == 0) | needed)

    def kv_goes(way, step):
        needed = (z >= step - 1) & (z < nz - 1) if way == 0 else ring(z + step - 1) < down_steps
        return (step <= last_offset[way]) & ((yl == 0) | needed)

    def kv_send(piece, way, step):
        return kv_copy(piece, way, step, step - 1, (up, down)[way])

    def kv_arrival(piece, way, step):
        return kv_copy(piece, way, step, step, (up, down)[way])

    proj = jnp.dot(nb[...], wg[...], preferred_element_type=jnp.float32)
    kt[z, :hw, :] = jnp.transpose(proj[:, :hw]).astype(jnp.bfloat16)
    kt[z, hw:hw + 16, :] = jnp.broadcast_to(sv[...].astype(jnp.float32), (16, rows)).astype(jnp.bfloat16)
    vb[z] = proj[:, hw:].astype(jnp.bfloat16)
    for way in (0, 1):
        @pl.when(kv_goes(way, 1))
        def _():
            for piece in range(4):
                kv_send(piece, way, 1).start()

    arrived(wgq.at[pl.ds(0, nz * depth), :], qy_r.at[0])
    qb[1] = jnp.dot(nb[...], wgq[...], preferred_element_type=jnp.float32).astype(jnp.bfloat16)
    query_copy = remote(qb.at[1], qb.at[0], x_s.at[0], x_r.at[0], across)

    @pl.when(yl == 1)
    def _():
        query_copy.start()

    slope = slopes[m]
    inv_scale = 1.0 / math.sqrt(hw)

    def attend(group, block):
        bias = kt[block, hw:hw + 16, :].astype(jnp.float32)[:1, :] * slope
        scores = jnp.dot(qb[group], kt[block, :hw, :], preferred_element_type=jnp.float32)
        scores = scores * inv_scale + bias
        reach = nz * rows if group == 0 else (z - block) * rows
        row = lax.broadcasted_iota(jnp.int32, scores.shape, 0)
        col = lax.broadcasted_iota(jnp.int32, scores.shape, 1)
        scores = jnp.where(col - row <= reach, scores, MASKED_SCORE)
        old = mb[group]
        new = jnp.maximum(old, jnp.max(scores, axis=1, keepdims=True))
        weights = jnp.exp(scores - jnp.concatenate([new] * (rows // hw), axis=1))
        factor = jnp.exp(old - new)
        total = lb[group] * factor
        for part in range(rows // hw):
            total = total + weights[:, part * hw:(part + 1) * hw]
        mb[group] = new
        lb[group] = total
        ab[group] = ab[group] * factor + jnp.dot(
            weights.astype(jnp.bfloat16), vb[block], preferred_element_type=jnp.float32
        )

    def wo_send(way, step):
        ref = wog.at[ring(z - (1 - 2 * way) * (step - 1))]
        return remote(ref, ref, p_s.at[way], p_r.at[way, step - 1], (up, down)[way])

    def wo_step(way, step):
        ref = wog.at[ring(z - (1 - 2 * way) * step)]
        remote(ref, ref, p_s.at[way], p_r.at[way, step - 1], up).wait_recv()
        remote(ref, ref, h_s.at[0], h_r.at[0], across).start()
        wo_send(way, step).wait_send()

        @pl.when(step < last_offset[way])
        def _():
            wo_send(way, step + 1).start()

    other_out = wog.at[z, 1 - yl]
    remote(other_out, other_out, o_s.at[0], o_r.at[0], across).wait_recv()

    @pl.when(yl == 1)
    def _():
        wo_send(0, 1).start()
        wo_send(1, 1).start()

    def kv_step(row, step, carry):
        before = step - 1
        comes = [kv_comes(way, step) if row else step <= last_offset[way] for way in (0, 1)]
        went = [kv_goes(way, step) if row else step <= last_offset[way] for way in (0, 1)]
        goes = [kv_goes(way, step + 1) if row else step + 1 <= last_offset[way] for way in (0, 1)]
        for index in range(4):
            for way in (0, 1):
                @pl.when(comes[way])
                def _():
                    kv_arrival(index, way, step).wait_recv()

                @pl.when(went[way])
                def _():
                    kv_send(index, way, step).wait_send()

                @pl.when(goes[way])
                def _():
                    kv_send(index, way, step + 1).start()

            way, group = index // 2, 1 - index % 2
            block = ring(z - (1 - 2 * way) * before)
            if group == 0 and row == 1:
                continue
            if index == 1:
                @pl.when(before == 0)
                def _():
                    query_copy.wait_recv()

            wanted = before >= 0 if group == 0 else block <= z
            if way == 1:
                wanted = wanted & (before >= 1) & (before <= down_steps)

            @pl.when(wanted)
            def _():
                attend(group, block)

        for way in (0, 1) if row else ():
            @pl.when(step <= last_offset[way])
            def _():
                wo_step(way, step)

        return carry

    @pl.when(yl == 0)
    def _():
        lax.fori_loop(1, up_steps + 2, functools.partial(kv_step, 0), 0)

    @pl.when(yl == 1)
    def _():
        lax.fori_loop(1, up_steps + 2, functools.partial(kv_step, 1), 0)


    out_copy = remote(ob.at[0], ob.at[1], x_s.at[1], x_r.at[1], across)
    stat_copy = remote(sb.at[0], sb.at[1], x_s.at[2], x_r.at[2], across)

    @pl.when(yl == 0)
    def _():
        total = jnp.sum(lb[0], axis=1, keepdims=True)
        ob[0] = (ab[0] / total).astype(jnp.bfloat16)
        out_copy.start()
        level = jnp.broadcast_to(mb[0] + jnp.log(total), (rows, hw))
        sb[0] = jnp.transpose(level)[:8, :]
        stat_copy.start()

    total = jnp.sum(lb[1], axis=1, keepdims=True)
    own = ab[1] / total

    @pl.when(yl == 0)
    def _():
        att[m] = own.astype(jnp.bfloat16)

    @pl.when(yl == 1)
    def _():
        own_level = jnp.broadcast_to(mb[1] + jnp.log(total), (rows, hw))
        stat_copy.wait_recv()
        other_level = jnp.transpose(jnp.broadcast_to(sb[1][:1, :], (hw, rows)))
        share = 1.0 / (1.0 + jnp.exp(other_level - own_level))
        out_copy.wait_recv()
        merged = own * share + ob[1].astype(jnp.float32) * (1.0 - share)
        att[m] = merged.astype(jnp.bfloat16)

    def att_copy(slot, a, b, sems, device):
        ref = att.at[slot]
        return remote(ref, ref, sems[0].at[0], sems[1].at[a * ny + b if sems is direct else 0], device)

    direct, handed = (a_s, a_r), (f_s, f_r)
    att_sends = [att_copy(m, a, b, direct, row_device(a, b, False)) for a, b in [(1, 0), (3, 0), (0, 1), (2, 0), (1, 1), (3, 1), (2, 1)]]
    att_sends += [att_copy(m, 0, 0, handed, sibling)]
    for copy in att_sends:
        copy.start()

    arrived(wg.at[pl.ds(0, (2 * nz - 1) * depth), :], w_s.at[0])
    arrived(wgq.at[pl.ds(0, (2 * nz - 1) * depth), :], q_s.at[0])
    arrived(xg.at[pl.ds(0, nm - 1)], tok_s.at[0])
    out_weight.wait_send()

    @pl.when(yl == 1)
    def _():
        arrived(wog.at[pl.ds(0, nz - 1)], h_s.at[0])

    @pl.when(yl == 0)
    def _():
        arrived(wog.at[pl.ds(0, nz - 1)], h_r.at[0])

    @pl.when(yl == 1)
    def _():
        query_copy.wait_send()

    @pl.when(yl == 0)
    def _():
        out_copy.wait_send()
        stat_copy.wait_send()

    per_head = hw // depth

    def project(head):
        first = head * per_head
        weight = wog[pl.ds(lax.rem(first, nz), per_head), lax.div(first, nz)].reshape(hw, hw)
        return jnp.dot(att[head], weight, preferred_element_type=jnp.float32)

    mixed = xg[m].astype(jnp.float32) + project(m)
    for a, b in [(1, 0), (3, 0), (0, 1), (2, 0), (1, 1), (3, 1), (2, 1)]:
        head = tile(-a, b, False)
        att_copy(head, a, b, direct, sibling).wait_recv()
        att_copy(head, a, b, handed, sibling).start()
        mixed = mixed + project(head)
    arrived(att.at[pl.ds(0, nx * ny)], f_r.at[0])
    for a, b in [(0, 0)] + others:
        mixed = mixed + project(tile(-a, b, True))
    out[...] = mixed.astype(jnp.bfloat16)

    arrived(att.at[pl.ds(0, nx * ny - 1)], a_s.at[0])
    arrived(att.at[pl.ds(0, nx * ny)], f_s.at[0])


def on_device(nz, nx, ny, tokens, norm_gain, w_query, w_key, w_value, w_out, head_slope, segment_ids):
    rows, hw = tokens.shape
    depth = w_query.shape[0]
    nm = nx * ny * 2
    steps = nz // 2 + 1
    vmem = pl.BlockSpec(memory_space=pltpu.VMEM)
    hbm = pl.BlockSpec(memory_space=pltpu.HBM)
    dma = pltpu.SemaphoreType.DMA
    return pl.pallas_call(
        functools.partial(kernel, nz, nx, ny),
        out_shape=jax.ShapeDtypeStruct((rows, hw), jnp.bfloat16),
        in_specs=[hbm] * 6 + [pl.BlockSpec(memory_space=pltpu.SMEM), hbm],
        out_specs=vmem,
        scratch_shapes=[
            pltpu.VMEM((nm, rows, hw), jnp.bfloat16),
            pltpu.VMEM((rows, nm * hw), jnp.bfloat16),
            pltpu.VMEM((2 * nz * depth, 2 * hw), jnp.bfloat16),
            pltpu.VMEM((2 * nz * depth, hw), jnp.bfloat16),
            pltpu.VMEM((nz, 2, depth, hw), jnp.bfloat16),
            pltpu.VMEM((1, nm * hw), jnp.float32),
            pltpu.VMEM((1, rows), jnp.int32),
            pltpu.VMEM((nz, hw + 16, rows), jnp.bfloat16),
            pltpu.VMEM((nz, rows, hw), jnp.bfloat16),
            pltpu.VMEM((2, rows, hw), jnp.bfloat16),
            pltpu.VMEM((2, rows, hw), jnp.float32),
            pltpu.VMEM((2, rows, hw), jnp.float32),
            pltpu.VMEM((2, rows, hw), jnp.float32),
            pltpu.VMEM((2, rows, hw), jnp.bfloat16),
            pltpu.VMEM((2, 8, rows), jnp.float32),
            pltpu.VMEM((nm, rows, hw), jnp.bfloat16),
            dma((7,)),
            dma((1,)), dma((1,)),
            dma((2,)), dma((2, steps - 1)),
            dma((1,)), dma((1,)),
            dma((1,)), dma((4,)),
            dma((1,)), dma((2, steps)),
            dma((1,)),
            dma((1,)), dma((2, steps)),
            dma((1,)),
            dma((4, 2)), dma((4, 2, steps - 1)),
            dma((3,)), dma((3,)),
            dma((1,)), dma((nx * ny,)),
            dma((1,)), dma((1,)),
        ],
        compiler_params=pltpu.CompilerParams(
            collective_id=0, has_side_effects=True, vmem_limit_bytes=60 << 20
        ),
        name="sublayer",
    )(
        tokens, norm_gain.reshape(1, -1), w_query, w_key, w_value, w_out, head_slope,
        segment_ids.reshape(1, -1),
    )


def solution(mesh):
    nz = mesh.shape["seq"] // 2
    ny = 2
    nx = mesh.shape["mp"] // (2 * ny)
    return jax.shard_map(
        functools.partial(on_device, nz, nx, ny),
        mesh=mesh,
        in_specs=(
            P("seq", "mp"), P(), P("seq", "mp"), P("seq", "mp"),
            P("seq", "mp"), P("seq", "mp"), P(), P("seq"),
        ),
        out_specs=P("seq", "mp"),
        check_vma=False,
    )
```

```python
import functools
import math

import jax
import jax.numpy as jnp
from jax import lax
from jax.experimental import pallas as pl
from jax.experimental.pallas import tpu as pltpu
from jax.sharding import PartitionSpec as P

EPSILON = 1e-05
MASKED_SCORE = -1e30
MESH = pl.DeviceIdType.MESH


def remote(src, dst, send, recv, device):
    return pltpu.make_async_remote_copy(
        src_ref=src, dst_ref=dst, send_sem=send, recv_sem=recv, device_id=device, device_id_type=MESH
    )


def kernel(
    nz, nx, ny, tok, gain, wq, wk, wv, wo, slopes, seg, out,
    xg, nb, wg, wgq, wog, gv, sv, kt, vb, qb, mb, lb, ab, ob, sb, att,
    l_s, o_s, o_r, p_s, p_r, h_s, h_r, tok_s, tok_r, w_s, w_r, wy_r, q_s, q_r, qy_r, kv_s, kv_r, x_s, x_r, a_s, a_r, f_s, f_r,
):
    rows, hw = tok.shape
    depth = wq.shape[0]
    nm = nx * ny * 2
    up_steps = nz // 2
    down_steps = nz - 1 - up_steps
    origin = {1: 0, 2: 0, 3: 2, 4: 2, 5: 4, 6: 4, 7: 6, 8: 6}
    hops = sorted(set(offset - origin[offset] for offset in origin))
    s = lax.axis_index("seq")
    m = lax.axis_index("mp")
    z = lax.rem(s, nz)
    yl = lax.div(s, nz)
    core = lax.rem(m, 2)
    yh = lax.rem(lax.div(m, 2), ny)
    x = lax.div(m, 2 * ny)

    def arrived(ref, sem):
        pltpu.make_async_copy(ref, ref, sem).wait()

    def ring(place):
        return lax.rem(place + nz, nz)

    def along(distance):
        return {"seq": yl * nz + ring(z + distance), "mp": m}

    up, down = along(1), along(-1)
    across = {"seq": (1 - yl) * nz + z, "mp": m}

    def tile(a, b, flip):
        return (lax.rem(x + a + nx, nx) * ny + lax.rem(yh + b, ny)) * 2 + (1 - core if flip else core)

    def row_device(a, b, flip):
        return {"seq": s, "mp": tile(a, b, flip)}

    sibling = row_device(0, 0, True)
    others = [(a, b) for a in range(nx) for b in range(ny) if a or b]

    barrier = pltpu.get_barrier_semaphore()
    greeted = [along(way * far) for far in hops for way in (1, -1)] + [across, sibling] + [row_device(a, b, False) for a, b in others]
    for device in greeted:
        pl.semaphore_signal(barrier, inc=1, device_id=device, device_id_type=MESH)

    def shard(buf, row, owner):
        start = pl.multiple_of((row * nz + ring(owner)) * depth, depth)
        return buf.at[pl.ds(start, depth), :]

    own_rows = pl.ds(pl.multiple_of(s * depth, depth), depth)
    own_out = wog.at[z, yl]
    loads = [
        pltpu.make_async_copy(wq, wgq.at[own_rows, :], l_s.at[0]),
        pltpu.make_async_copy(wk, wg.at[own_rows, pl.ds(0, hw)], l_s.at[1]),
        pltpu.make_async_copy(wv, wg.at[own_rows, pl.ds(hw, hw)], l_s.at[2]),
        pltpu.make_async_copy(tok, xg.at[m], l_s.at[3]),
        pltpu.make_async_copy(wo, own_out, l_s.at[4]),
        pltpu.make_async_copy(gain, gv, l_s.at[5]),
        pltpu.make_async_copy(seg, sv, l_s.at[6]),
    ]
    for load in loads:
        load.start()
    mb[...] = jnp.full(mb.shape, MASKED_SCORE, jnp.float32)
    lb[...] = jnp.zeros(lb.shape, jnp.float32)
    ab[...] = jnp.zeros(ab.shape, jnp.float32)
    for load in loads:
        load.wait()
    pl.semaphore_wait(barrier, len(greeted))

    key_value, queries = (wg, w_s, w_r, wy_r), (wgq, q_s, q_r, qy_r)

    def w_send(side, way, offset):
        buf, sent, came, _ = side
        sign = 1 - 2 * way
        ref = shard(buf, yl, z - sign * origin[offset])
        return remote(ref, ref, sent.at[0], came.at[way, offset], along(sign * (offset - origin[offset])))

    def w_hand(side, way, offset):
        buf, sent, _, handed = side
        ref = shard(buf, yl, z - (1 - 2 * way) * offset)
        return remote(ref, ref, sent.at[0], handed.at[0], across)

    def w_event(offset, sides=None):
        for side in sides or (key_value, queries):
            for way in (0, 1):
                if offset <= last_offset[way]:
                    arrived(shard(side[0], yl, z - (1 - 2 * way) * offset), side[2].at[way, offset])
                    for later in range(last_offset[way], offset, -1):
                        if origin[later] == offset:
                            w_send(side, way, later).start()
                    w_hand(side, way, offset).start()

    last_offset = (up_steps, down_steps)
    for first in range(1, up_steps + 1):
        if origin[first] == 0:
            for side in (key_value, queries):
                for way in (0, 1):
                    w_send(side, way, first).start()
    for side in (key_value, queries):
        w_hand(side, 0, 0).start()

    def tok_copy(slot, a, b, flip, device):
        ref = xg.at[slot]
        kind = 3 if flip else 2 * b if a else 1
        return remote(ref, ref, tok_s.at[0], tok_r.at[kind], device)

    tok_sends = [tok_copy(m, 0, 1, 0, row_device(0, 1, False))]
    tok_sends += [tok_copy(m, a, 0, 0, row_device(a, 0, False)) for a in range(1, nx)]
    tok_sends += [tok_copy(m, 0, 0, 1, sibling)]
    for copy in tok_sends:
        copy.start()
    out_weight = remote(own_out, own_out, o_s.at[0], o_r.at[0], across)
    out_weight.start()

    def tok_pass(a, b):
        later = []
        if (a, b) == (0, 1):
            later += [tok_copy(tile(0, 1, False), c, 1, 0, row_device(c, 0, False)) for c in range(1, nx)]
        later += [tok_copy(tile(-a, b, False), a, b, 1, sibling)]
        for copy in later:
            copy.start()

    w_event(2, (key_value,))
    w_event(1, (key_value,))
    arrived(xg.at[0], tok_r.at[1])
    tok_pass(0, 1)
    w_event(2, (queries,))
    w_event(1, (queries,))
    arrived(xg.at[pl.ds(0, nx - 1)], tok_r.at[0])
    for a in range(1, nx):
        tok_pass(a, 0)
    w_event(4, (key_value,))
    w_event(3, (key_value,))
    w_event(4, (queries,))
    w_event(3, (queries,))
    arrived(xg.at[pl.ds(0, nx - 1)], tok_r.at[2])
    for a in range(1, nx):
        tok_pass(a, 1)
    w_event(6, (key_value,))
    w_event(5, (key_value,))
    w_event(6, (queries,))
    w_event(5, (queries,))
    arrived(xg.at[pl.ds(0, nx * ny)], tok_r.at[3])
    square = jnp.zeros((rows, hw), jnp.float32)
    for h in range(nm):
        part = xg[h].astype(jnp.float32)
        square = square + part * part
    mean = jnp.sum(square, axis=1, keepdims=True) * (1.0 / (nm * hw))
    scale = jnp.broadcast_to(lax.rsqrt(mean + EPSILON), (rows, hw))
    for h in range(nm):
        part = xg[h].astype(jnp.float32) * scale * gv[:, h * hw:(h + 1) * hw]
        nb[:, h * hw:(h + 1) * hw] = part.astype(jnp.bfloat16)

    w_event(8, (key_value,))
    w_event(7, (key_value,))
    w_event(8, (queries,))
    w_event(7, (queries,))
    arrived(wg.at[pl.ds(0, nz * depth), :], wy_r.at[0])

    half = hw // 2
    middle = rows // 2
    pieces = (
        (kt, 0, half), (kt, half, half + 16), (vb, 0, middle), (vb, middle, middle),
    )

    def kv_copy(piece, way, step, offset, device):
        buf, start, length = pieces[piece]
        ref = buf.at[ring(z - (1 - 2 * way) * offset), pl.ds(start, length), :]
        return remote(ref, ref, kv_s.at[piece, way], kv_r.at[piece, way, step - 1], device)

    def kv_comes(way, step):
        needed = z >= step if way == 0 else ring(z + step) < down_steps
        return (step <= last_offset[way]) & ((yl == 0) | needed)

    def kv_goes(way, step):
        needed = (z >= step - 1) & (z < nz - 1) if way == 0 else ring(z + step - 1) < down_steps
        return (step <= last_offset[way]) & ((yl == 0) | needed)

    def kv_send(piece, way, step):
        return kv_copy(piece, way, step, step - 1, (up, down)[way])

    def kv_arrival(piece, way, step):
        return kv_copy(piece, way, step, step, (up, down)[way])

    proj = jnp.dot(nb[...], wg[...], preferred_element_type=jnp.float32)
    kt[z, :hw, :] = jnp.transpose(proj[:, :hw]).astype(jnp.bfloat16)
    kt[z, hw:hw + 16, :] = jnp.broadcast_to(sv[...].astype(jnp.float32), (16, rows)).astype(jnp.bfloat16)
    vb[z] = proj[:, hw:].astype(jnp.bfloat16)
    for way in (0, 1):
        @pl.when(kv_goes(way, 1))
        def _():
            for piece in range(4):
                kv_send(piece, way, 1).start()

    arrived(wgq.at[pl.ds(0, nz * depth), :], qy_r.at[0])
    qb[1] = jnp.dot(nb[...], wgq[...], preferred_element_type=jnp.float32).astype(jnp.bfloat16)
    query_copy = remote(qb.at[1], qb.at[0], x_s.at[0], x_r.at[0], across)

    @pl.when(yl == 1)
    def _():
        query_copy.start()

    slope = slopes[m]
    inv_scale = 1.0 / math.sqrt(hw)

    def attend(group, block):
        bias = kt[block, hw:hw + 16, :].astype(jnp.float32)[:1, :] * slope
        scores = jnp.dot(qb[group], kt[block, :hw, :], preferred_element_type=jnp.float32)
        scores = scores * inv_scale + bias
        reach = nz * rows if group == 0 else (z - block) * rows
        row = lax.broadcasted_iota(jnp.int32, scores.shape, 0)
        col = lax.broadcasted_iota(jnp.int32, scores.shape, 1)
        scores = jnp.where(col - row <= reach, scores, MASKED_SCORE)
        old = mb[group]
        new = jnp.maximum(old, jnp.max(scores, axis=1, keepdims=True))
        weights = jnp.exp(scores - jnp.concatenate([new] * (rows // hw), axis=1))
        factor = jnp.exp(old - new)
        total = lb[group] * factor
        for part in range(rows // hw):
            total = total + weights[:, part * hw:(part + 1) * hw]
        mb[group] = new
        lb[group] = total
        ab[group] = ab[group] * factor + jnp.dot(
            weights.astype(jnp.bfloat16), vb[block], preferred_element_type=jnp.float32
        )

    def wo_send(way, step):
        ref = wog.at[ring(z - (1 - 2 * way) * (step - 1))]
        return remote(ref, ref, p_s.at[way], p_r.at[way, step - 1], (up, down)[way])

    def wo_step(way, step):
        ref = wog.at[ring(z - (1 - 2 * way) * step)]
        remote(ref, ref, p_s.at[way], p_r.at[way, step - 1], up).wait_recv()
        remote(ref, ref, h_s.at[0], h_r.at[0], across).start()
        wo_send(way, step).wait_send()

        @pl.when(step < last_offset[way])
        def _():
            wo_send(way, step + 1).start()

    other_out = wog.at[z, 1 - yl]
    remote(other_out, other_out, o_s.at[0], o_r.at[0], across).wait_recv()

    @pl.when(yl == 1)
    def _():
        wo_send(0, 1).start()
        wo_send(1, 1).start()

    def kv_step(row, step, carry):
        before = step - 1
        comes = [kv_comes(way, step) if row else step <= last_offset[way] for way in (0, 1)]
        went = [kv_goes(way, step) if row else step <= last_offset[way] for way in (0, 1)]
        goes = [kv_goes(way, step + 1) if row else step + 1 <= last_offset[way] for way in (0, 1)]
        for index in range(4):
            for way in (0, 1):
                @pl.when(comes[way])
                def _():
                    kv_arrival(index, way, step).wait_recv()

                @pl.when(went[way])
                def _():
                    kv_send(index, way, step).wait_send()

                @pl.when(goes[way])
                def _():
                    kv_send(index, way, step + 1).start()

            way, group = index // 2, 1 - index % 2
            block = ring(z - (1 - 2 * way) * before)
            if group == 0 and row == 1:
                continue
            if index == 1:
                @pl.when(before == 0)
                def _():
                    query_copy.wait_recv()

            wanted = before >= 0 if group == 0 else block <= z
            if way == 1:
                wanted = wanted & (before >= 1) & (before <= down_steps)

            @pl.when(wanted)
            def _():
                attend(group, block)

        for way in (0, 1) if row else ():
            @pl.when(step <= last_offset[way])
            def _():
                wo_step(way, step)

        return carry

    @pl.when(yl == 0)
    def _():
        lax.fori_loop(1, up_steps + 2, functools.partial(kv_step, 0), 0)

    @pl.when(yl == 1)
    def _():
        lax.fori_loop(1, up_steps + 2, functools.partial(kv_step, 1), 0)


    out_copy = remote(ob.at[0], ob.at[1], x_s.at[1], x_r.at[1], across)
    stat_copy = remote(sb.at[0], sb.at[1], x_s.at[2], x_r.at[2], across)

    @pl.when(yl == 0)
    def _():
        total = jnp.sum(lb[0], axis=1, keepdims=True)
        ob[0] = (ab[0] / total).astype(jnp.bfloat16)
        out_copy.start()
        level = jnp.broadcast_to(mb[0] + jnp.log(total), (rows, hw))
        sb[0] = jnp.transpose(level)[:8, :]
        stat_copy.start()

    total = jnp.sum(lb[1], axis=1, keepdims=True)
    own = ab[1] / total

    @pl.when(yl == 0)
    def _():
        att[m] = own.astype(jnp.bfloat16)

    @pl.when(yl == 1)
    def _():
        own_level = jnp.broadcast_to(mb[1] + jnp.log(total), (rows, hw))
        stat_copy.wait_recv()
        other_level = jnp.transpose(jnp.broadcast_to(sb[1][:1, :], (hw, rows)))
        share = 1.0 / (1.0 + jnp.exp(other_level - own_level))
        out_copy.wait_recv()
        merged = own * share + ob[1].astype(jnp.float32) * (1.0 - share)
        att[m] = merged.astype(jnp.bfloat16)

    def att_copy(slot, a, b, sems, device):
        ref = att.at[slot]
        return remote(ref, ref, sems[0].at[0], sems[1].at[a * ny + b if sems is direct else 0], device)

    direct, handed = (a_s, a_r), (f_s, f_r)
    att_sends = [att_copy(m, a, b, direct, row_device(a, b, False)) for a, b in [(1, 0), (3, 0), (0, 1), (2, 0), (1, 1), (3, 1), (2, 1)]]
    att_sends += [att_copy(m, 0, 0, handed, sibling)]
    for copy in att_sends:
        copy.start()

    arrived(wg.at[pl.ds(0, (2 * nz - 1) * depth), :], w_s.at[0])
    arrived(wgq.at[pl.ds(0, (2 * nz - 1) * depth), :], q_s.at[0])
    arrived(xg.at[pl.ds(0, nm - 1)], tok_s.at[0])
    out_weight.wait_send()

    @pl.when(yl == 1)
    def _():
        arrived(wog.at[pl.ds(0, nz - 1)], h_s.at[0])

    @pl.when(yl == 0)
    def _():
        arrived(wog.at[pl.ds(0, nz - 1)], h_r.at[0])

    @pl.when(yl == 1)
    def _():
        query_copy.wait_send()

    @pl.when(yl == 0)
    def _():
        out_copy.wait_send()
        stat_copy.wait_send()

    per_head = hw // depth

    def project(head):
        first = head * per_head
        weight = wog[pl.ds(lax.rem(first, nz), per_head), lax.div(first, nz)].reshape(hw, hw)
        return jnp.dot(att[head], weight, preferred_element_type=jnp.float32)

    mixed = xg[m].astype(jnp.float32) + project(m)
    for a, b in [(1, 0), (3, 0), (0, 1), (2, 0), (1, 1), (3, 1), (2, 1)]:
        head = tile(-a, b, False)
        att_copy(head, a, b, direct, sibling).wait_recv()
        att_copy(head, a, b, handed, sibling).start()
        mixed = mixed + project(head)
    arrived(att.at[pl.ds(0, nx * ny)], f_r.at[0])
    for a, b in [(0, 0)] + others:
        mixed = mixed + project(tile(-a, b, True))
    out[...] = mixed.astype(jnp.bfloat16)

    arrived(att.at[pl.ds(0, nx * ny - 1)], a_s.at[0])
    arrived(att.at[pl.ds(0, nx * ny)], f_s.at[0])


def on_device(nz, nx, ny, tokens, norm_gain, w_query, w_key, w_value, w_out, head_slope, segment_ids):
    rows, hw = tokens.shape
    depth = w_query.shape[0]
    nm = nx * ny * 2
    steps = nz // 2 + 1
    vmem = pl.BlockSpec(memory_space=pltpu.VMEM)
    hbm = pl.BlockSpec(memory_space=pltpu.HBM)
    dma = pltpu.SemaphoreType.DMA
    return pl.pallas_call(
        functools.partial(kernel, nz, nx, ny),
        out_shape=jax.ShapeDtypeStruct((rows, hw), jnp.bfloat16),
        in_specs=[hbm] * 6 + [pl.BlockSpec(memory_space=pltpu.SMEM), hbm],
        out_specs=vmem,
        scratch_shapes=[
            pltpu.VMEM((nm, rows, hw), jnp.bfloat16),
            pltpu.VMEM((rows, nm * hw), jnp.bfloat16),
            pltpu.VMEM((2 * nz * depth, 2 * hw), jnp.bfloat16),
            pltpu.VMEM((2 * nz * depth, hw), jnp.bfloat16),
            pltpu.VMEM((nz, 2, depth, hw), jnp.bfloat16),
            pltpu.VMEM((1, nm * hw), jnp.float32),
            pltpu.VMEM((1, rows), jnp.int32),
            pltpu.VMEM((nz, hw + 16, rows), jnp.bfloat16),
            pltpu.VMEM((nz, rows, hw), jnp.bfloat16),
            pltpu.VMEM((2, rows, hw), jnp.bfloat16),
            pltpu.VMEM((2, rows, hw), jnp.float32),
            pltpu.VMEM((2, rows, hw), jnp.float32),
            pltpu.VMEM((2, rows, hw), jnp.float32),
            pltpu.VMEM((2, rows, hw), jnp.bfloat16),
            pltpu.VMEM((2, 8, rows), jnp.float32),
            pltpu.VMEM((nm, rows, hw), jnp.bfloat16),
            dma((7,)),
            dma((1,)), dma((1,)),
            dma((2,)), dma((2, steps - 1)),
            dma((1,)), dma((1,)),
            dma((1,)), dma((4,)),
            dma((1,)), dma((2, steps)),
            dma((1,)),
            dma((1,)), dma((2, steps)),
            dma((1,)),
            dma((4, 2)), dma((4, 2, steps - 1)),
            dma((3,)), dma((3,)),
            dma((1,)), dma((nx * ny,)),
            dma((1,)), dma((1,)),
        ],
        compiler_params=pltpu.CompilerParams(
            collective_id=0, has_side_effects=True, vmem_limit_bytes=60 << 20
        ),
        name="sublayer",
    )(
        tokens, norm_gain.reshape(1, -1), w_query, w_key, w_value, w_out, head_slope,
        segment_ids.reshape(1, -1),
    )


def solution(mesh):
    nz = mesh.shape["seq"] // 2
    ny = 2
    nx = mesh.shape["mp"] // (2 * ny)
    return jax.shard_map(
        functools.partial(on_device, nz, nx, ny),
        mesh=mesh,
        in_specs=(
            P("seq", "mp"), P(), P("seq", "mp"), P("seq", "mp"),
            P("seq", "mp"), P("seq", "mp"), P(), P("seq"),
        ),
        out_specs=P("seq", "mp"),
        check_vma=False,
    )
```

```python
import functools
import math

import jax
import jax.numpy as jnp
from jax import lax
from jax.experimental import pallas as pl
from jax.experimental.pallas import tpu as pltpu
from jax.sharding import PartitionSpec as P

EPSILON = 1e-05
MASKED_SCORE = -1e30
MESH = pl.DeviceIdType.MESH


def remote(src, dst, send, recv, device):
    return pltpu.make_async_remote_copy(
        src_ref=src, dst_ref=dst, send_sem=send, recv_sem=recv, device_id=device, device_id_type=MESH
    )


def kernel(
    nz, nx, ny, tok, gain, wq, wk, wv, wo, slopes, seg, out,
    xg, nb, wg, wgq, wog, gv, sv, kt, vb, qb, mb, lb, ab, ob, sb, att,
    l_s, o_s, o_r, p_s, p_r, h_s, h_r, tok_s, tok_r, w_s, w_r, wy_r, q_s, q_r, qy_r, kv_s, kv_r, x_s, x_r, a_s, a_r, f_s, f_r,
):
    rows, hw = tok.shape
    depth = wq.shape[0]
    nm = nx * ny * 2
    up_steps = nz // 2
    down_steps = nz - 1 - up_steps
    origin = {1: 0, 2: 0, 3: 2, 4: 2, 5: 4, 6: 4, 7: 6, 8: 6}
    hops = sorted(set(offset - origin[offset] for offset in origin))
    s = lax.axis_index("seq")
    m = lax.axis_index("mp")
    z = lax.rem(s, nz)
    yl = lax.div(s, nz)
    core = lax.rem(m, 2)
    yh = lax.rem(lax.div(m, 2), ny)
    x = lax.div(m, 2 * ny)

    def arrived(ref, sem):
        pltpu.make_async_copy(ref, ref, sem).wait()

    def ring(place):
        return lax.rem(place + nz, nz)

    def along(distance):
        return {"seq": yl * nz + ring(z + distance), "mp": m}

    up, down = along(1), along(-1)
    across = {"seq": (1 - yl) * nz + z, "mp": m}

    def tile(a, b, flip):
        return (lax.rem(x + a + nx, nx) * ny + lax.rem(yh + b, ny)) * 2 + (1 - core if flip else core)

    def row_device(a, b, flip):
        return {"seq": s, "mp": tile(a, b, flip)}

    sibling = row_device(0, 0, True)
    others = [(a, b) for a in range(nx) for b in range(ny) if a or b]

    barrier = pltpu.get_barrier_semaphore()
    greeted = [along(way * far) for far in hops for way in (1, -1)] + [across, sibling] + [row_device(a, b, False) for a, b in others]
    for device in greeted:
        pl.semaphore_signal(barrier, inc=1, device_id=device, device_id_type=MESH)

    def shard(buf, row, owner):
        start = pl.multiple_of((row * nz + ring(owner)) * depth, depth)
        return buf.at[pl.ds(start, depth), :]

    own_rows = pl.ds(pl.multiple_of(s * depth, depth), depth)
    own_out = wog.at[z, yl]
    loads = [
        pltpu.make_async_copy(wq, wgq.at[own_rows, :], l_s.at[0]),
        pltpu.make_async_copy(wk, wg.at[own_rows, pl.ds(0, hw)], l_s.at[1]),
        pltpu.make_async_copy(wv, wg.at[own_rows, pl.ds(hw, hw)], l_s.at[2]),
        pltpu.make_async_copy(tok, xg.at[m], l_s.at[3]),
        pltpu.make_async_copy(wo, own_out, l_s.at[4]),
        pltpu.make_async_copy(gain, gv, l_s.at[5]),
        pltpu.make_async_copy(seg, sv, l_s.at[6]),
    ]
    for load in loads:
        load.start()
    mb[...] = jnp.full(mb.shape, MASKED_SCORE, jnp.float32)
    lb[...] = jnp.zeros(lb.shape, jnp.float32)
    ab[...] = jnp.zeros(ab.shape, jnp.float32)
    for load in loads:
        load.wait()
    pl.semaphore_wait(barrier, len(greeted))

    key_value, queries = (wg, w_s, w_r, wy_r), (wgq, q_s, q_r, qy_r)

    def w_send(side, way, offset):
        buf, sent, came, _ = side
        sign = 1 - 2 * way
        ref = shard(buf, yl, z - sign * origin[offset])
        return remote(ref, ref, sent.at[0], came.at[way, offset], along(sign * (offset - origin[offset])))

    def w_hand(side, way, offset):
        buf, sent, _, handed = side
        ref = shard(buf, yl, z - (1 - 2 * way) * offset)
        return remote(ref, ref, sent.at[0], handed.at[0], across)

    def w_event(offset, sides=None):
        for side in sides or (key_value, queries):
            for way in (0, 1):
                if offset <= last_offset[way]:
                    arrived(shard(side[0], yl, z - (1 - 2 * way) * offset), side[2].at[way, offset])
                    for later in range(last_offset[way], offset, -1):
                        if origin[later] == offset:
                            w_send(side, way, later).start()
                    w_hand(side, way, offset).start()

    last_offset = (up_steps, down_steps)
    for first in range(up_steps, 0, -1):
        if origin[first] == 0:
            for side in (key_value, queries):
                for way in (0, 1):
                    w_send(side, way, first).start()
    for side in (key_value, queries):
        w_hand(side, 0, 0).start()

    def tok_copy(slot, a, b, flip, device):
        ref = xg.at[slot]
        kind = 3 if flip else 2 * b if a else 1
        return remote(ref, ref, tok_s.at[0], tok_r.at[kind], device)

    tok_sends = [tok_copy(m, 0, 1, 0, row_device(0, 1, False))]
    tok_sends += [tok_copy(m, a, 0, 0, row_device(a, 0, False)) for a in range(1, nx)]
    tok_sends += [tok_copy(m, 0, 0, 1, sibling)]
    for copy in tok_sends:
        copy.start()
    out_weight = remote(own_out, own_out, o_s.at[0], o_r.at[0], across)
    out_weight.start()

    def tok_pass(a, b):
        later = []
        if (a, b) == (0, 1):
            later += [tok_copy(tile(0, 1, False), c, 1, 0, row_device(c, 0, False)) for c in range(1, nx)]
        later += [tok_copy(tile(-a, b, False), a, b, 1, sibling)]
        for copy in later:
            copy.start()

    w_event(2, (key_value,))
    w_event(1, (key_value,))
    arrived(xg.at[0], tok_r.at[1])
    tok_pass(0, 1)
    w_event(2, (queries,))
    w_event(1, (queries,))
    arrived(xg.at[pl.ds(0, nx - 1)], tok_r.at[0])
    for a in range(1, nx):
        tok_pass(a, 0)
    w_event(4, (key_value,))
    w_event(3, (key_value,))
    w_event(4, (queries,))
    w_event(3, (queries,))
    arrived(xg.at[pl.ds(0, nx - 1)], tok_r.at[2])
    for a in range(1, nx):
        tok_pass(a, 1)
    w_event(6, (key_value,))
    w_event(5, (key_value,))
    w_event(6, (queries,))
    w_event(5, (queries,))
    arrived(xg.at[pl.ds(0, nx * ny)], tok_r.at[3])
    square = jnp.zeros((rows, hw), jnp.float32)
    for h in range(nm):
        part = xg[h].astype(jnp.float32)
        square = square + part * part
    mean = jnp.sum(square, axis=1, keepdims=True) * (1.0 / (nm * hw))
    scale = jnp.broadcast_to(lax.rsqrt(mean + EPSILON), (rows, hw))
    for h in range(nm):
        part = xg[h].astype(jnp.float32) * scale * gv[:, h * hw:(h + 1) * hw]
        nb[:, h * hw:(h + 1) * hw] = part.astype(jnp.bfloat16)

    w_event(8, (key_value,))
    w_event(7, (key_value,))
    w_event(8, (queries,))
    w_event(7, (queries,))
    arrived(wg.at[pl.ds(0, nz * depth), :], wy_r.at[0])

    half = hw // 2
    middle = rows // 2
    pieces = (
        (kt, 0, half), (kt, half, half + 16), (vb, 0, middle), (vb, middle, middle),
    )

    def kv_copy(piece, way, step, offset, device):
        buf, start, length = pieces[piece]
        ref = buf.at[ring(z - (1 - 2 * way) * offset), pl.ds(start, length), :]
        return remote(ref, ref, kv_s.at[piece, way], kv_r.at[piece, way, step - 1], device)

    def kv_comes(way, step):
        needed = z >= step if way == 0 else ring(z + step) < down_steps
        return (step <= last_offset[way]) & ((yl == 0) | needed)

    def kv_goes(way, step):
        needed = (z >= step - 1) & (z < nz - 1) if way == 0 else ring(z + step - 1) < down_steps
        return (step <= last_offset[way]) & ((yl == 0) | needed)

    def kv_send(piece, way, step):
        return kv_copy(piece, way, step, step - 1, (up, down)[way])

    def kv_arrival(piece, way, step):
        return kv_copy(piece, way, step, step, (up, down)[way])

    proj = jnp.dot(nb[...], wg[...], preferred_element_type=jnp.float32)
    kt[z, :hw, :] = jnp.transpose(proj[:, :hw]).astype(jnp.bfloat16)
    kt[z, hw:hw + 16, :] = jnp.broadcast_to(sv[...].astype(jnp.float32), (16, rows)).astype(jnp.bfloat16)
    vb[z] = proj[:, hw:].astype(jnp.bfloat16)
    for way in (0, 1):
        @pl.when(kv_goes(way, 1))
        def _():
            for piece in range(4):
                kv_send(piece, way, 1).start()

    arrived(wgq.at[pl.ds(0, nz * depth), :], qy_r.at[0])
    qb[1] = jnp.dot(nb[...], wgq[...], preferred_element_type=jnp.float32).astype(jnp.bfloat16)
    query_copy = remote(qb.at[1], qb.at[0], x_s.at[0], x_r.at[0], across)

    @pl.when(yl == 1)
    def _():
        query_copy.start()

    slope = slopes[m]
    inv_scale = 1.0 / math.sqrt(hw)

    def attend(group, block):
        bias = kt[block, hw:hw + 16, :].astype(jnp.float32)[:1, :] * slope
        scores = jnp.dot(qb[group], kt[block, :hw, :], preferred_element_type=jnp.float32)
        scores = scores * inv_scale + bias
        reach = nz * rows if group == 0 else (z - block) * rows
        row = lax.broadcasted_iota(jnp.int32, scores.shape, 0)
        col = lax.broadcasted_iota(jnp.int32, scores.shape, 1)
        scores = jnp.where(col - row <= reach, scores, MASKED_SCORE)
        old = mb[group]
        new = jnp.maximum(old, jnp.max(scores, axis=1, keepdims=True))
        weights = jnp.exp(scores - jnp.concatenate([new] * (rows // hw), axis=1))
        factor = jnp.exp(old - new)
        total = lb[group] * factor
        for part in range(rows // hw):
            total = total + weights[:, part * hw:(part + 1) * hw]
        mb[group] = new
        lb[group] = total
        ab[group] = ab[group] * factor + jnp.dot(
            weights.astype(jnp.bfloat16), vb[block], preferred_element_type=jnp.float32
        )

    def wo_send(way, step):
        ref = wog.at[ring(z - (1 - 2 * way) * (step - 1))]
        return remote(ref, ref, p_s.at[way], p_r.at[way, step - 1], (up, down)[way])

    def wo_step(way, step):
        ref = wog.at[ring(z - (1 - 2 * way) * step)]
        remote(ref, ref, p_s.at[way], p_r.at[way, step - 1], up).wait_recv()
        remote(ref, ref, h_s.at[0], h_r.at[0], across).start()
        wo_send(way, step).wait_send()

        @pl.when(step < last_offset[way])
        def _():
            wo_send(way, step + 1).start()

    other_out = wog.at[z, 1 - yl]
    remote(other_out, other_out, o_s.at[0], o_r.at[0], across).wait_recv()

    @pl.when(yl == 1)
    def _():
        wo_send(0, 1).start()
        wo_send(1, 1).start()

    def kv_step(row, step, carry):
        before = step - 1
        comes = [kv_comes(way, step) if row else step <= last_offset[way] for way in (0, 1)]
        went = [kv_goes(way, step) if row else step <= last_offset[way] for way in (0, 1)]
        goes = [kv_goes(way, step + 1) if row else step + 1 <= last_offset[way] for way in (0, 1)]
        for index in range(4):
            for way in (0, 1):
                @pl.when(comes[way])
                def _():
                    kv_arrival(index, way, step).wait_recv()

                @pl.when(went[way])
                def _():
                    kv_send(index, way, step).wait_send()

                @pl.when(goes[way])
                def _():
                    kv_send(index, way, step + 1).start()

            way, group = index // 2, 1 - index % 2
            block = ring(z - (1 - 2 * way) * before)
            if group == 0 and row == 1:
                continue
            if index == 1:
                @pl.when(before == 0)
                def _():
                    query_copy.wait_recv()

            wanted = before >= 0 if group == 0 else block <= z
            if way == 1:
                wanted = wanted & (before >= 1) & (before <= down_steps)

            @pl.when(wanted)
            def _():
                attend(group, block)

        for way in (0, 1) if row else ():
            @pl.when(step <= last_offset[way])
            def _():
                wo_step(way, step)

        return carry

    @pl.when(yl == 0)
    def _():
        lax.fori_loop(1, up_steps + 2, functools.partial(kv_step, 0), 0)

    @pl.when(yl == 1)
    def _():
        lax.fori_loop(1, up_steps + 2, functools.partial(kv_step, 1), 0)


    out_copy = remote(ob.at[0], ob.at[1], x_s.at[1], x_r.at[1], across)
    stat_copy = remote(sb.at[0], sb.at[1], x_s.at[2], x_r.at[2], across)

    @pl.when(yl == 0)
    def _():
        total = jnp.sum(lb[0], axis=1, keepdims=True)
        ob[0] = (ab[0] / total).astype(jnp.bfloat16)
        out_copy.start()
        level = jnp.broadcast_to(mb[0] + jnp.log(total), (rows, hw))
        sb[0] = jnp.transpose(level)[:8, :]
        stat_copy.start()

    total = jnp.sum(lb[1], axis=1, keepdims=True)
    own = ab[1] / total

    @pl.when(yl == 0)
    def _():
        att[m] = own.astype(jnp.bfloat16)

    @pl.when(yl == 1)
    def _():
        own_level = jnp.broadcast_to(mb[1] + jnp.log(total), (rows, hw))
        stat_copy.wait_recv()
        other_level = jnp.transpose(jnp.broadcast_to(sb[1][:1, :], (hw, rows)))
        share = 1.0 / (1.0 + jnp.exp(other_level - own_level))
        out_copy.wait_recv()
        merged = own * share + ob[1].astype(jnp.float32) * (1.0 - share)
        att[m] = merged.astype(jnp.bfloat16)

    def att_copy(slot, a, b, sems, device):
        ref = att.at[slot]
        return remote(ref, ref, sems[0].at[0], sems[1].at[a * ny + b if sems is direct else 0], device)

    direct, handed = (a_s, a_r), (f_s, f_r)
    att_sends = [att_copy(m, a, b, direct, row_device(a, b, False)) for a, b in [(1, 0), (3, 0), (0, 1), (2, 0), (1, 1), (3, 1), (2, 1)]]
    att_sends += [att_copy(m, 0, 0, handed, sibling)]
    for copy in att_sends:
        copy.start()

    arrived(wg.at[pl.ds(0, (2 * nz - 1) * depth), :], w_s.at[0])
    arrived(wgq.at[pl.ds(0, (2 * nz - 1) * depth), :], q_s.at[0])
    arrived(xg.at[pl.ds(0, nm - 1)], tok_s.at[0])
    out_weight.wait_send()

    @pl.when(yl == 1)
    def _():
        arrived(wog.at[pl.ds(0, nz - 1)], h_s.at[0])

    @pl.when(yl == 0)
    def _():
        arrived(wog.at[pl.ds(0, nz - 1)], h_r.at[0])

    @pl.when(yl == 1)
    def _():
        query_copy.wait_send()

    @pl.when(yl == 0)
    def _():
        out_copy.wait_send()
        stat_copy.wait_send()

    per_head = hw // depth

    def project(head):
        first = head * per_head
        weight = wog[pl.ds(lax.rem(first, nz), per_head), lax.div(first, nz)].reshape(hw, hw)
        return jnp.dot(att[head], weight, preferred_element_type=jnp.float32)

    mixed = xg[m].astype(jnp.float32) + project(m)
    for a, b in [(1, 0), (3, 0), (0, 1), (2, 0), (1, 1), (3, 1), (2, 1)]:
        head = tile(-a, b, False)
        att_copy(head, a, b, direct, sibling).wait_recv()
        att_copy(head, a, b, handed, sibling).start()
        mixed = mixed + project(head)
    arrived(att.at[pl.ds(0, nx * ny)], f_r.at[0])
    for a, b in [(0, 0)] + others:
        mixed = mixed + project(tile(-a, b, True))
    out[...] = mixed.astype(jnp.bfloat16)

    arrived(att.at[pl.ds(0, nx * ny - 1)], a_s.at[0])
    arrived(att.at[pl.ds(0, nx * ny)], f_s.at[0])


def on_device(nz, nx, ny, tokens, norm_gain, w_query, w_key, w_value, w_out, head_slope, segment_ids):
    rows, hw = tokens.shape
    depth = w_query.shape[0]
    nm = nx * ny * 2
    steps = nz // 2 + 1
    vmem = pl.BlockSpec(memory_space=pltpu.VMEM)
    hbm = pl.BlockSpec(memory_space=pltpu.HBM)
    dma = pltpu.SemaphoreType.DMA
    return pl.pallas_call(
        functools.partial(kernel, nz, nx, ny),
        out_shape=jax.ShapeDtypeStruct((rows, hw), jnp.bfloat16),
        in_specs=[hbm] * 6 + [pl.BlockSpec(memory_space=pltpu.SMEM), hbm],
        out_specs=vmem,
        scratch_shapes=[
            pltpu.VMEM((nm, rows, hw), jnp.bfloat16),
            pltpu.VMEM((rows, nm * hw), jnp.bfloat16),
            pltpu.VMEM((2 * nz * depth, 2 * hw), jnp.bfloat16),
            pltpu.VMEM((2 * nz * depth, hw), jnp.bfloat16),
            pltpu.VMEM((nz, 2, depth, hw), jnp.bfloat16),
            pltpu.VMEM((1, nm * hw), jnp.float32),
            pltpu.VMEM((1, rows), jnp.int32),
            pltpu.VMEM((nz, hw + 16, rows), jnp.bfloat16),
            pltpu.VMEM((nz, rows, hw), jnp.bfloat16),
            pltpu.VMEM((2, rows, hw), jnp.bfloat16),
            pltpu.VMEM((2, rows, hw), jnp.float32),
            pltpu.VMEM((2, rows, hw), jnp.float32),
            pltpu.VMEM((2, rows, hw), jnp.float32),
            pltpu.VMEM((2, rows, hw), jnp.bfloat16),
            pltpu.VMEM((2, 8, rows), jnp.float32),
            pltpu.VMEM((nm, rows, hw), jnp.bfloat16),
            dma((7,)),
            dma((1,)), dma((1,)),
            dma((2,)), dma((2, steps - 1)),
            dma((1,)), dma((1,)),
            dma((1,)), dma((4,)),
            dma((1,)), dma((2, steps)),
            dma((1,)),
            dma((1,)), dma((2, steps)),
            dma((1,)),
            dma((4, 2)), dma((4, 2, steps - 1)),
            dma((3,)), dma((3,)),
            dma((1,)), dma((nx * ny,)),
            dma((1,)), dma((1,)),
        ],
        compiler_params=pltpu.CompilerParams(
            collective_id=0, has_side_effects=True, vmem_limit_bytes=60 << 20
        ),
        name="sublayer",
    )(
        tokens, norm_gain.reshape(1, -1), w_query, w_key, w_value, w_out, head_slope,
        segment_ids.reshape(1, -1),
    )


def solution(mesh):
    nz = mesh.shape["seq"] // 2
    ny = 2
    nx = mesh.shape["mp"] // (2 * ny)
    return jax.shard_map(
        functools.partial(on_device, nz, nx, ny),
        mesh=mesh,
        in_specs=(
            P("seq", "mp"), P(), P("seq", "mp"), P("seq", "mp"),
            P("seq", "mp"), P("seq", "mp"), P(), P("seq"),
        ),
        out_specs=P("seq", "mp"),
        check_vma=False,
    )
```
